256 devices in a mesh: filt: 8 (over y, core), rows: 16 (over x_lo, z), rep: 2 (over x_hi).
Axes of the slice: x: 4 (x_hi: 2, x_lo: 2; x = x_hi * 2 + x_lo), y: 4, z: 8, core: 2. Of those that a mesh axis runs over, the one named last changes fastest.
Arguments:
- features: bfloat16 [2, 64, 64, 2048], P('rep', 'rows', None, 'filt'), may hold values from -6 to 6
- kernel: bfloat16 [3, 3, 2048, 2048], P(None, None, 'rows', 'filt'), may hold values from -0.046875 to 0.046875
- cotangent: bfloat16 [2, 32, 32, 2048], P('rep', 'rows', None, 'filt'), may hold values from -6 to 6
Outputs:
- pooled: bfloat16 [2, 32, 32, 2048], P('rep', 'rows', None, 'filt')
- input_grad: bfloat16 [2, 64, 64, 2048], P('rep', 'rows', None, 'filt')
- kernel_grad: float32 [3, 3, 2048, 2048], P(None, None, 'rows', 'filt')
The draws below stay inside these ranges and needn't reach their ends.
All inputs are finite; a program needn't handle non-finite values.
Results may differ from the reference program's by a relative error of at most 0.0032.
Values may be sent and summed in bfloat16 or wider, within the bound.
No kernel may reach another device: no remote copies, remote signals or barrier semaphores. Data moves between devices by JAX's collectives and lax.ppermute only.
A program may use at most 128 MiB of HBM per device.

```python
import jax
import jax.numpy as jnp
from jax import lax

CHANNELS = 2048
HEIGHT = 64
WIDTH = 64
BATCH = 2


def level_of(rng, shape, shards, least, top_value):
    level = 1.0
    for axis_at, parts in shards:
        heights = jax.random.uniform(jax.random.fold_in(jax.random.fold_in(rng, 6), axis_at), (parts,), jnp.float32, least / len(shards), top_value / len(shards))
        level = level * jnp.repeat(jnp.exp(heights), shape[axis_at] // parts).reshape((-1,) + (1,) * (len(shape) - 1 - axis_at))
    return level


def noise(own_key, dims, scale, bound, cuts=(), held_as=jnp.bfloat16):
    values = jax.random.normal(own_key, dims, jnp.float32) * scale
    if len(cuts) > 0:
        values = level_of(own_key, dims, cuts, -0.22, 0.18) * values
    return jnp.clip(values, min=-bound, max=bound).astype(held_as)


def setup_inputs(seed: int = 0) -> dict:
    streams_of = jax.random.split(jax.random.key(seed), 4)
    features = noise(streams_of[0], (BATCH, HEIGHT, WIDTH, CHANNELS), 1.0, 6.0, ((0, 2), (1, 16), (3, 8)))
    kernel = noise(streams_of[1], (3, 3, CHANNELS, CHANNELS), (9 * CHANNELS) ** -0.5, 0.046875, ((2, 16), (3, 8)))
    cotangent = noise(streams_of[2], (BATCH, HEIGHT // 2, WIDTH // 2, CHANNELS), 1.0, 6.0, ((0, 2), (1, 16), (3, 8)))
    return {"features": features, "kernel": kernel, "cotangent": cotangent}


def silu_slope(values):
    logistic = jax.nn.sigmoid(values)
    return logistic * (1.0 + values * (1.0 - logistic))


def reference(features, kernel, cotangent):
    values = features.astype(jnp.float32)
    activated = jax.nn.silu(values).astype(jnp.bfloat16)
    images, height, width, channels = features.shape
    framed = jnp.pad(activated, ((0, 0), (1, 1), (1, 1), (0, 0)))
    tokens_all = images * height * width
    conv_sum = jnp.zeros((tokens_all, channels), jnp.float32)
    for row_tap in range(3):
        for col_tap in range(3):
            window = framed[:, row_tap:row_tap + height, col_tap:col_tap + width, :].reshape(tokens_all, channels)
            conv_sum = conv_sum + jnp.dot(window, kernel[row_tap, col_tap], preferred_element_type=jnp.float32)
    pre_pool = values + conv_sum.reshape(images, height, width, channels)
    pooled = pre_pool.reshape(images, height // 2, 2, width // 2, 2, channels).mean(axis=(2, 4)).astype(jnp.bfloat16)
    up_grad = (jnp.repeat(jnp.repeat(cotangent.astype(jnp.float32), 2, axis=1), 2, axis=2) * 0.25).astype(jnp.bfloat16)
    grad_framed = jnp.pad(up_grad, ((0, 0), (1, 1), (1, 1), (0, 0)))
    back_sum = jnp.zeros((tokens_all, channels), jnp.float32)
    for row_tap in range(3):
        for col_tap in range(3):
            grad_window = grad_framed[:, 2 - row_tap:2 - row_tap + height, 2 - col_tap:2 - col_tap + width, :].reshape(tokens_all, channels)
            back_sum = back_sum + lax.dot_general(grad_window, kernel[row_tap, col_tap], (((1,), (1,)), ((), ())), preferred_element_type=jnp.float32)
    act_grad = back_sum.reshape(images, height, width, channels)
    input_grad = (up_grad.astype(jnp.float32) + act_grad * silu_slope(values)).astype(jnp.bfloat16)
    grad_flat = up_grad.reshape(tokens_all, channels)
    tap_sums = []
    for row_tap in range(3):
        for col_tap in range(3):
            window = framed[:, row_tap:row_tap + height, col_tap:col_tap + width, :].reshape(tokens_all, channels)
            tap_sums.append(lax.dot_general(window, grad_flat, (((0,), (0,)), ((), ())), preferred_element_type=jnp.float32))
    kernel_grad = jnp.stack(tap_sums).reshape(3, 3, channels, channels)
    return pooled, input_grad, kernel_grad
```

```python
import jax
import jax.numpy as jnp
from jax import lax
from jax.sharding import PartitionSpec as P

AXES = ("filt", "rows", "rep")


def swap_tiles(same, other):
    sizes = [lax.axis_size(axis) for axis in AXES]
    stay, cross = [], []
    for f in range(sizes[0]):
        for r in range(sizes[1]):
            for g in range(sizes[2]):
                a, h = r // 2, r % 2
                source = (f * sizes[1] + r) * sizes[2] + g
                stay.append((source, (a * sizes[1] + 2 * f + h) * sizes[2] + g))
                cross.append((source, (a * sizes[1] + 2 * f + 1 - h) * sizes[2] + g))
    return lax.ppermute(same, AXES, stay), lax.ppermute(other, AXES, cross)


def local(features, kernel, cotangent):
    tile_rows, columns, local_channels = features.shape[1:]
    half = local_channels // 2
    odd = lax.axis_index("rows") % 2 == 1
    filt_count = lax.axis_size("filt")
    row_count = lax.axis_size("rows")
    height = tile_rows * row_count
    kernel_flat = kernel.reshape(9 * half, local_channels)

    packed = jnp.concatenate(
        [
            features.reshape(tile_rows * columns, local_channels),
            cotangent.reshape(tile_rows * columns // 4, local_channels),
        ],
        axis=0,
    )
    low, high = packed[:, :half], packed[:, half:]
    got_same, got_other = swap_tiles(jnp.where(odd, high, low), jnp.where(odd, low, high))
    tiles = jnp.stack([jnp.where(odd, got_other, got_same), jnp.where(odd, got_same, got_other)])
    tokens = tile_rows * columns
    values = tiles[:, :tokens].reshape(2 * tile_rows, columns, half).astype(jnp.float32)
    own_cot = tiles[:, tokens:].reshape(tile_rows, columns // 2, half).astype(jnp.float32)
    own_up = jnp.repeat(jnp.repeat(own_cot, 2, axis=0), 2, axis=1) * 0.25
    logistic = jax.nn.sigmoid(values)
    activated = jax.nn.silu(values).astype(jnp.bfloat16)
    act = lax.all_gather(activated, "filt", axis=0, tiled=True)

    copies = jnp.broadcast_to(cotangent, (row_count,) + cotangent.shape[1:])
    cot = lax.all_to_all(copies, "rows", 0, 0, tiled=True).reshape(height // 2, columns // 2, local_channels)

    up = jnp.repeat(jnp.repeat(cot, 2, axis=0), 2, axis=1)[None]
    back = lax.conv_general_dilated(
        up,
        kernel[::-1, ::-1],
        (1, 1),
        ((1, 1), (1, 1)),
        dimension_numbers=("NHWC", "HWOI", "NHWC"),
        preferred_element_type=jnp.float32,
    )
    back = (back[0] * 0.25).astype(jnp.bfloat16)
    back = lax.all_to_all(back, "filt", 0, 0, tiled=True)
    act_grad = back.reshape(filt_count, 2 * tile_rows, columns, half).astype(jnp.float32).sum(axis=0)
    slope = logistic * (1.0 + values * (1.0 - logistic))
    input_grad = (own_up + act_grad * slope).astype(jnp.bfloat16).reshape(2, tokens, half)
    sent = jnp.where(odd, input_grad[1], input_grad[0]), jnp.where(odd, input_grad[0], input_grad[1])
    got_same, got_other = swap_tiles(*sent)
    input_grad = jnp.concatenate(
        [jnp.where(odd, got_other, got_same), jnp.where(odd, got_same, got_other)], axis=-1
    ).reshape(features.shape)

    framed = jnp.pad(act, ((1, 1), (1, 1), (0, 0))).astype(jnp.float32)
    boxes = framed[:-1] + framed[1:]
    boxes = boxes[:, :-1] + boxes[:, 1:]
    coarse = boxes.astype(jnp.bfloat16)
    fine = (boxes - coarse.astype(jnp.float32)).astype(jnp.bfloat16)

    def windows(source):
        return jnp.concatenate(
            [
                source[p : p + height : 2, q : q + columns : 2].reshape(height * columns // 4, half)
                for p in range(3)
                for q in range(3)
            ],
            axis=1,
        )

    coarse, fine = windows(coarse), windows(fine)
    cot_flat = cot.reshape(height * columns // 4, local_channels)
    kernel_term = lax.dot_general(
        coarse, cot_flat, (((0,), (0,)), ((), ())), preferred_element_type=jnp.float32
    ) * 0.25
    arrived = lax.ppermute(kernel_term.astype(jnp.bfloat16), "rep", [(0, 1), (1, 0)])
    kernel_grad = (kernel_term + arrived.astype(jnp.float32)).reshape(kernel.shape)

    conv = jnp.dot(coarse, kernel_flat, preferred_element_type=jnp.float32)
    conv = conv + jnp.dot(fine, kernel_flat, preferred_element_type=jnp.float32)
    conv = conv.astype(jnp.bfloat16).reshape(height // 2, columns // 2, local_channels)
    conv = lax.all_to_all(conv, "rows", 0, 0, tiled=True)
    conv = conv.reshape(row_count, tile_rows // 2, columns // 2, local_channels).astype(jnp.float32).sum(axis=0)
    cells = features.astype(jnp.float32).reshape(tile_rows // 2, 2, columns // 2, 2, local_channels)
    pooled = ((cells.sum(axis=(1, 3)) + conv) * 0.25).astype(jnp.bfloat16)[None]
    return (pooled, input_grad, kernel_grad)


def solution(mesh):
    tiles = P("rep", "rows", None, "filt")
    weights = P(None, None, "rows", "filt")
    return jax.shard_map(
        local,
        mesh=mesh,
        in_specs=(tiles, weights, tiles),
        out_specs=(tiles, tiles, weights),
        check_vma=False,
    )
```

```python
import jax
import jax.numpy as jnp
from jax import lax
from jax.experimental import pallas as pl
from jax.experimental.pallas import tpu as pltpu
from jax.sharding import PartitionSpec as P

AXES = ("filt", "rows", "rep")
VMEM = pl.BlockSpec(memory_space=pltpu.VMEM)
SMEM = pl.BlockSpec(memory_space=pltpu.SMEM)
F32 = jnp.float32
BF16 = jnp.bfloat16


def call(body, outs, scratch, scalars, *args):
    return pl.pallas_call(
        body,
        out_shape=[jax.ShapeDtypeStruct(shape, dtype) for shape, dtype in outs],
        in_specs=[SMEM] * scalars + [VMEM] * (len(args) - scalars),
        out_specs=[VMEM] * len(outs),
        scratch_shapes=scratch,
        compiler_params=pltpu.CompilerParams(vmem_limit_bytes=48 << 20),
        name=body.__name__,
    )(*args)


def swap_tiles(pair):
    sizes = [lax.axis_size(axis) for axis in AXES]
    stay, cross = [], []
    for f in range(sizes[0]):
        for r in range(sizes[1]):
            for g in range(sizes[2]):
                a, h = r // 2, r % 2
                source = (f * sizes[1] + r) * sizes[2] + g
                stay.append((source, (a * sizes[1] + 2 * f + h) * sizes[2] + g))
                cross.append((source, (a * sizes[1] + 2 * f + 1 - h) * sizes[2] + g))
    return lax.ppermute(pair[0], AXES, stay), lax.ppermute(pair[1], AXES, cross)


def split_tile(odd_ref, feat_ref, cot_ref, same_ref, other_ref, copies_ref, cells_ref, wide_ref):
    odd = odd_ref[0] == 1
    rows, columns, channels = feat_ref.shape
    half, cells = channels // 2, columns // 2
    for part in range(2):
        wide_ref[part] = feat_ref[:, :, part * half : (part + 1) * half].astype(F32)
    for m in range(rows // 2):
        totals = [jnp.zeros((cells, half), F32)] * 2
        for a in range(2):
            for b in range(2):
                low, high = (wide_ref[part, 2 * m + a, pl.ds(b, cells, stride=2), :] for part in range(2))
                totals = [totals[0] + low, totals[1] + high]
                same_ref[4 * m + 2 * a + b] = jnp.where(odd, high, low).astype(BF16)
                other_ref[4 * m + 2 * a + b] = jnp.where(odd, low, high).astype(BF16)
        cells_ref[m, :, :half] = totals[0]
        cells_ref[m, :, half:] = totals[1]
        grad = cot_ref[m].astype(F32)
        low, high = grad[:, :half], grad[:, half:]
        same_ref[2 * rows + m] = jnp.where(odd, high, low).astype(BF16)
        other_ref[2 * rows + m] = jnp.where(odd, low, high).astype(BF16)
    for k in range(copies_ref.shape[0]):
        copies_ref[k] = cot_ref[...]


def activate(odd_ref, same_ref, other_ref, act_ref, slope_ref, up_ref):
    odd = odd_ref[0] == 1
    count, cells, half = same_ref.shape
    planes = act_ref.shape[0] // 2
    same, other = same_ref[...].astype(F32), other_ref[...].astype(F32)
    first, second = jnp.where(odd, other, same), jnp.where(odd, same, other)
    for t, tile in enumerate((first, second)):
        values = tile[:planes]
        logistic = 1.0 / (1.0 + jnp.exp(-values))
        act_ref[t * planes : (t + 1) * planes] = (values * logistic).astype(BF16)
        slope_ref[t * planes : (t + 1) * planes] = logistic * (1.0 + values * (1.0 - logistic))
        up_ref[t * (planes // 4) : (t + 1) * (planes // 4)] = tile[planes:] * 0.25


def back_conv(cot_ref, kernel_ref, out_ref, left_ref, right_ref):
    height, cells, channels = cot_ref.shape
    half = out_ref.shape[-1]
    tokens = height * cells
    column = lax.broadcasted_iota(jnp.int32, (tokens, channels), 0) % cells
    wide = cot_ref[...].astype(F32).reshape(tokens, channels)
    before = jnp.where(column == 0, 0.0, pltpu.roll(wide, 1, 0)).astype(BF16)
    after = jnp.where(column == cells - 1, 0.0, pltpu.roll(wide, tokens - 1, 0)).astype(BF16)
    blank = jnp.zeros((cells, 4 * channels), BF16)
    left_ref[0:cells] = blank
    left_ref[tokens + cells : tokens + 2 * cells] = blank
    middle = pl.ds(cells, tokens)
    center = cot_ref[...].reshape(tokens, channels)
    left_ref[middle, 0:channels] = center
    left_ref[middle, channels : 2 * channels] = center
    left_ref[middle, 2 * channels : 3 * channels] = before
    left_ref[middle, 3 * channels : 4 * channels] = after
    empty = jnp.zeros((half, channels), BF16)
    for p in range(3):
        taps = [kernel_ref[(3 * p + q) * half : (3 * p + q + 1) * half, :] for q in range(3)]
        blocks = ((taps[0], taps[1]), (taps[1], taps[2]), (taps[2], empty), (empty, taps[0]))
        for k, block in enumerate(blocks):
            for b in range(2):
                right_ref[p, b * half : (b + 1) * half, k * channels : (k + 1) * channels] = block[b]
    for a in range(2):
        total = None
        for p in range(3):
            start = cells * (1 + ((0, 0, -1), (1, 0, 0))[a][p])
            term = lax.dot_general(
                left_ref[start : start + tokens, :],
                right_ref[p],
                (((1,), (1,)), ((), ())),
                preferred_element_type=F32,
            )
            total = term if total is None else total + term
        total = (total * 0.25).astype(BF16).reshape(height, cells, 2 * half)
        for b in range(2):
            out_ref[:, a, b] = total[:, :, b * half : (b + 1) * half]


def forward_and_kernel(act_ref, cot_ref, kernel_ref, conv_ref, keep_ref, send_ref, coarse_ref, fine_ref):
    height, _, _, cells, half = act_ref.shape
    column = lax.broadcasted_iota(jnp.int32, (cells, half), 0)

    def plane(i, a, b):
        return act_ref[i, a, b].astype(F32)

    def put(i, p, even, odd):
        before = jnp.where(column == 0, 0.0, pltpu.roll(odd, 1, 0))
        after = jnp.where(column == cells - 1, 0.0, pltpu.roll(even, cells - 1, 0))
        rows = pl.ds(pl.multiple_of(i * cells, cells), cells)
        return rows, (before + even, even + odd, odd + after)

    def store(rows, p, sums):
        for q, box in enumerate(sums):
            coarse = box.astype(BF16)
            lanes = slice((3 * p + q) * half, (3 * p + q + 1) * half)
            coarse_ref[rows, lanes] = coarse
            fine_ref[rows, lanes] = (box - coarse.astype(F32)).astype(BF16)

    rows, sums = put(0, 0, plane(0, 0, 0), plane(0, 0, 1))
    store(rows, 0, sums)
    rows, sums = put(height - 1, 2, plane(height - 1, 1, 0), plane(height - 1, 1, 1))
    store(rows, 2, sums)

    def whole(i, _):
        rows, sums = put(i, 1, plane(i, 0, 0) + plane(i, 1, 0), plane(i, 0, 1) + plane(i, 1, 1))
        store(rows, 1, sums)
        return 0

    def between(i, _):
        rows, sums = put(
            i, 0, plane(i - 1, 1, 0) + plane(i, 0, 0), plane(i - 1, 1, 1) + plane(i, 0, 1)
        )
        store(rows, 0, sums)
        store(pl.ds(pl.multiple_of((i - 1) * cells, cells), cells), 2, sums)
        return 0

    lax.fori_loop(0, height, whole, 0, unroll=4)
    lax.fori_loop(1, height, between, 0, unroll=4)

    tokens = height * cells
    grad = lax.dot_general(
        coarse_ref[...],
        cot_ref[...].reshape(tokens, -1),
        (((0,), (0,)), ((), ())),
        preferred_element_type=F32,
    ) * 0.25
    keep_ref[...] = grad
    send_ref[...] = grad.astype(BF16)
    conv = jnp.dot(coarse_ref[...], kernel_ref[...], preferred_element_type=F32)
    conv = conv + jnp.dot(fine_ref[...], kernel_ref[...], preferred_element_type=F32)
    conv_ref[...] = conv.astype(BF16).reshape(conv_ref.shape)


def input_side(odd_ref, back_ref, slope_ref, up_ref, same_ref, other_ref):
    odd = odd_ref[0] == 1
    planes = same_ref.shape[0]
    grads = []
    for t in range(2):
        block = slice(t * planes, (t + 1) * planes)
        total = back_ref[0, block].astype(F32)
        for k in range(1, back_ref.shape[0]):
            total = total + back_ref[k, block].astype(F32)
        total = total * slope_ref[block]
        up = up_ref[t * (planes // 4) : (t + 1) * (planes // 4)]
        grads.append([total[k] + up[k // 4] for k in range(planes)])
    for k in range(planes):
        same_ref[k] = jnp.where(odd, grads[1][k], grads[0][k]).astype(BF16)
        other_ref[k] = jnp.where(odd, grads[0][k], grads[1][k]).astype(BF16)


def join_tile(odd_ref, same_ref, other_ref, out_ref, low_ref, high_ref):
    odd = odd_ref[0] == 1
    rows, columns, channels = out_ref.shape
    half = channels // 2
    for k in range(2 * rows):
        row, b = 2 * (k // 4) + (k // 2) % 2, k % 2
        same, other = same_ref[k].astype(F32), other_ref[k].astype(F32)
        low_ref[row, pl.ds(b, columns // 2, stride=2), :] = jnp.where(odd, other, same)
        high_ref[row, pl.ds(b, columns // 2, stride=2), :] = jnp.where(odd, same, other)
    out_ref[:, :, :half] = low_ref[...].astype(BF16)
    out_ref[:, :, half:] = high_ref[...].astype(BF16)


def local(features, kernel, cotangent):
    tile_rows, columns, channels = features.shape[1:]
    half, cells = channels // 2, columns // 2
    filt_count, row_count = lax.axis_size("filt"), lax.axis_size("rows")
    height = tile_rows * row_count // 2
    odd = (lax.axis_index("rows") % 2).astype(jnp.int32).reshape(1)
    kernel_flat = kernel.reshape(9 * half, channels)
    planes = 2 * tile_rows

    packed = planes + tile_rows // 2
    same, other, copies, cell_sums = call(
        split_tile,
        [
            ((packed, cells, half), BF16),
            ((packed, cells, half), BF16),
            ((row_count,) + cotangent.shape[1:], BF16),
            ((tile_rows // 2, cells, channels), F32),
        ],
        [pltpu.VMEM((2, tile_rows, columns, half), F32)],
        1,
        odd,
        features[0],
        cotangent[0],
    )
    same, other = swap_tiles((same, other))
    cot = lax.all_to_all(copies, "rows", 0, 0, tiled=True).reshape(height, cells, channels)
    act, slope, up = call(
        activate,
        [
            ((2 * planes, cells, half), BF16),
            ((2 * planes, cells, half), F32),
            ((tile_rows, cells, half), F32),
        ],
        [],
        1,
        odd,
        same,
        other,
    )
    act = lax.all_gather(act, "filt", axis=0, tiled=True).reshape(height, 2, 2, cells, half)

    (back,) = call(
        back_conv,
        [((height, 2, 2, cells, half), BF16)],
        [
            pltpu.VMEM(((height + 2) * cells, 4 * channels), BF16),
            pltpu.VMEM((3, 2 * half, 4 * channels), BF16),
        ],
        0,
        cot,
        kernel_flat,
    )
    back = lax.all_to_all(back, "filt", 0, 0, tiled=True)
    conv, kernel_term, outgoing = call(
        forward_and_kernel,
        [
            ((height, cells, channels), BF16),
            ((9 * half, channels), F32),
            ((9 * half, channels), BF16),
        ],
        [
            pltpu.VMEM((height * cells, 9 * half), BF16),
            pltpu.VMEM((height * cells, 9 * half), BF16),
        ],
        0,
        act,
        cot,
        kernel_flat,
    )
    arrived = lax.ppermute(outgoing, "rep", [(0, 1), (1, 0)])
    conv = lax.all_to_all(conv, "rows", 0, 0, tiled=True)

    same, other = call(
        input_side,
        [((planes, cells, half), BF16), ((planes, cells, half), BF16)],
        [],
        1,
        odd,
        back.reshape(filt_count, 2 * planes, cells, half),
        slope,
        up,
    )
    same, other = swap_tiles((same, other))
    (input_grad,) = call(
        join_tile,
        [(features.shape[1:], BF16)],
        [pltpu.VMEM((tile_rows, columns, half), F32)] * 2,
        1,
        odd,
        same,
        other,
    )
    kernel_grad = (kernel_term + arrived.astype(F32)).reshape(kernel.shape)
    conv = conv.reshape(row_count, tile_rows // 2, cells, channels).astype(F32).sum(axis=0)
    pooled = ((cell_sums + conv) * 0.25).astype(BF16)
    return (pooled[None], input_grad[None], kernel_grad)


def solution(mesh):
    tiles = P("rep", "rows", None, "filt")
    weights = P(None, None, "rows", "filt")
    return jax.shard_map(
        local,
        mesh=mesh,
        in_specs=(tiles, weights, tiles),
        out_specs=(tiles, tiles, weights),
        check_vma=False,
    )
```

```python
import jax
import jax.numpy as jnp
from jax import lax
from jax.experimental import pallas as pl
from jax.experimental.pallas import tpu as pltpu
from jax.sharding import PartitionSpec as P

AXES = ("filt", "rows", "rep")
VMEM = pl.BlockSpec(memory_space=pltpu.VMEM)
SMEM = pl.BlockSpec(memory_space=pltpu.SMEM)
F32 = jnp.float32
BF16 = jnp.bfloat16


def call(body, outs, scratch, scalars, *args):
    return pl.pallas_call(
        body,
        out_shape=[jax.ShapeDtypeStruct(shape, dtype) for shape, dtype in outs],
        in_specs=[SMEM] * scalars + [VMEM] * (len(args) - scalars),
        out_specs=[VMEM] * len(outs),
        scratch_shapes=scratch,
        compiler_params=pltpu.CompilerParams(vmem_limit_bytes=48 << 20),
        name=body.__name__,
    )(*args)


def swap_tiles(pair):
    sizes = [lax.axis_size(axis) for axis in AXES]
    stay, cross = [], []
    for f in range(sizes[0]):
        for r in range(sizes[1]):
            for g in range(sizes[2]):
                a, h = r // 2, r % 2
                source = (f * sizes[1] + r) * sizes[2] + g
                stay.append((source, (a * sizes[1] + 2 * f + h) * sizes[2] + g))
                cross.append((source, (a * sizes[1] + 2 * f + 1 - h) * sizes[2] + g))
    return lax.ppermute(pair[0], AXES, stay), lax.ppermute(pair[1], AXES, cross)


def to_y(block, step):
    count = lax.axis_size("filt")
    return lax.ppermute(block, "filt", [(i, (i + 2 * step) % count) for i in range(count)])


def to_core(block):
    return lax.ppermute(block, "filt", [(i, i ^ 1) for i in range(lax.axis_size("filt"))])


def split_tile(place_ref, feat_ref, cot_ref, same_ref, other_ref, copies_ref, cells_ref, wide_ref):
    odd = place_ref[0] == 1
    rows, columns, channels = feat_ref.shape
    half, cells = channels // 2, columns // 2
    for part in range(2):
        wide_ref[part] = feat_ref[:, :, part * half : (part + 1) * half].astype(F32)
    for m in range(rows // 2):
        totals = [jnp.zeros((cells, half), F32)] * 2
        for a in range(2):
            for b in range(2):
                low, high = (wide_ref[part, 2 * m + a, pl.ds(b, cells, stride=2), :] for part in range(2))
                totals = [totals[0] + low, totals[1] + high]
                same_ref[4 * m + 2 * a + b] = jnp.where(odd, high, low).astype(BF16)
                other_ref[4 * m + 2 * a + b] = jnp.where(odd, low, high).astype(BF16)
        cells_ref[m, :, :half] = totals[0]
        cells_ref[m, :, half:] = totals[1]
        grad = cot_ref[m].astype(F32)
        low, high = grad[:, :half], grad[:, half:]
        same_ref[2 * rows + m] = jnp.where(odd, high, low).astype(BF16)
        other_ref[2 * rows + m] = jnp.where(odd, low, high).astype(BF16)
    for k in range(copies_ref.shape[0]):
        copies_ref[k] = cot_ref[...]


def activate(place_ref, same_ref, other_ref, act_ref, slope_ref, up_ref):
    odd = place_ref[0] == 1
    count, cells, half = same_ref.shape
    planes = act_ref.shape[0] // 2
    same, other = same_ref[...].astype(F32), other_ref[...].astype(F32)
    first, second = jnp.where(odd, other, same), jnp.where(odd, same, other)
    for t, tile in enumerate((first, second)):
        values = tile[:planes]
        logistic = 1.0 / (1.0 + jnp.exp(-values))
        act_ref[t * planes : (t + 1) * planes] = (values * logistic).astype(BF16)
        slope_ref[t * planes : (t + 1) * planes] = logistic * (1.0 + values * (1.0 - logistic))
        up_ref[t * (planes // 4) : (t + 1) * (planes // 4)] = tile[planes:] * 0.25


def back_conv(place_ref, cot_ref, kernel_ref, cross_ref, keep_ref, left_ref, right_ref, sum_ref):
    height, cells, channels = cot_ref.shape
    half = keep_ref.shape[-1]
    tokens = height * cells
    column = lax.broadcasted_iota(jnp.int32, (tokens, channels), 0) % cells
    wide = cot_ref[...].astype(F32).reshape(tokens, channels)
    before = jnp.where(column == 0, 0.0, pltpu.roll(wide, 1, 0)).astype(BF16)
    after = jnp.where(column == cells - 1, 0.0, pltpu.roll(wide, tokens - 1, 0)).astype(BF16)
    blank = jnp.zeros((cells, 4 * channels), BF16)
    left_ref[0:cells] = blank
    left_ref[tokens + cells : tokens + 2 * cells] = blank
    middle = pl.ds(cells, tokens)
    center = cot_ref[...].reshape(tokens, channels)
    left_ref[middle, 0:channels] = center
    left_ref[middle, channels : 2 * channels] = center
    left_ref[middle, 2 * channels : 3 * channels] = before
    left_ref[middle, 3 * channels : 4 * channels] = after
    empty = jnp.zeros((half, channels), BF16)
    for p in range(3):
        taps = [kernel_ref[(3 * p + q) * half : (3 * p + q + 1) * half, :] for q in range(3)]
        blocks = ((taps[0], taps[1]), (taps[1], taps[2]), (taps[2], empty), (empty, taps[0]))
        for k, block in enumerate(blocks):
            for b in range(2):
                right_ref[p, b * half : (b + 1) * half, k * channels : (k + 1) * channels] = block[b]
    for a in range(2):
        total = None
        for p in range(3):
            start = cells * (1 + ((0, 0, -1), (1, 0, 0))[a][p])
            term = lax.dot_general(
                left_ref[start : start + tokens, :],
                right_ref[p],
                (((1,), (1,)), ((), ())),
                preferred_element_type=F32,
            )
            total = term if total is None else total + term
        total = (total * 0.25).reshape(height, cells, 2 * half)
        for b in range(2):
            sum_ref[:, 2 * a + b] = total[:, :, b * half : (b + 1) * half]
    steps = keep_ref.shape[0]
    y, core = place_ref[1], place_ref[2]
    group = height // (2 * steps)
    for step in range(steps):
        pair = 2 * ((y + step) % steps)
        keep_ref[step] = sum_ref[pl.ds((pair + core) * group, group)].reshape(keep_ref.shape[1:])
        cross_ref[step] = sum_ref[pl.ds((pair + 1 - core) * group, group)].reshape(keep_ref.shape[1:]).astype(BF16)


def add_cores(keep_ref, cross_ref, own_ref, *out_refs):
    own_ref[...] = keep_ref[0] + cross_ref[0].astype(F32)
    for step, out_ref in enumerate(out_refs, 1):
        out_ref[...] = (keep_ref[step] + cross_ref[step].astype(F32)).astype(BF16)


def forward_and_kernel(place_ref, *refs):
    chunks, (cot_ref, kernel_ref, conv_ref, keep_ref, send_ref, act_ref, coarse_ref, fine_ref) = refs[:-8], refs[-8:]
    steps = len(chunks) // 2
    planes, cells, half = chunks[0].shape
    height = act_ref.shape[0] // 4
    y, core = place_ref[1], place_ref[2]
    for step in range(steps):
        pair = 2 * ((y + steps - step) % steps)
        act_ref[pl.ds((pair + core) * planes, planes)] = chunks[2 * step][...]
        act_ref[pl.ds((pair + 1 - core) * planes, planes)] = chunks[2 * step + 1][...]
    column = lax.broadcasted_iota(jnp.int32, (cells, half), 0)

    def plane(i, a, b):
        return act_ref[4 * i + 2 * a + b].astype(F32)

    def put(i, p, even, odd):
        before = jnp.where(column == 0, 0.0, pltpu.roll(odd, 1, 0))
        after = jnp.where(column == cells - 1, 0.0, pltpu.roll(even, cells - 1, 0))
        rows = pl.ds(pl.multiple_of(i * cells, cells), cells)
        return rows, (before + even, even + odd, odd + after)

    def store(rows, p, sums):
        for q, box in enumerate(sums):
            coarse = box.astype(BF16)
            lanes = slice((3 * p + q) * half, (3 * p + q + 1) * half)
            coarse_ref[rows, lanes] = coarse
            fine_ref[rows, lanes] = (box - coarse.astype(F32)).astype(BF16)

    rows, sums = put(0, 0, plane(0, 0, 0), plane(0, 0, 1))
    store(rows, 0, sums)
    rows, sums = put(height - 1, 2, plane(height - 1, 1, 0), plane(height - 1, 1, 1))
    store(rows, 2, sums)

    def whole(i, _):
        rows, sums = put(i, 1, plane(i, 0, 0) + plane(i, 1, 0), plane(i, 0, 1) + plane(i, 1, 1))
        store(rows, 1, sums)
        return 0

    def between(i, _):
        rows, sums = put(
            i, 0, plane(i - 1, 1, 0) + plane(i, 0, 0), plane(i - 1, 1, 1) + plane(i, 0, 1)
        )
        store(rows, 0, sums)
        store(pl.ds(pl.multiple_of((i - 1) * cells, cells), cells), 2, sums)
        return 0

    lax.fori_loop(0, height, whole, 0, unroll=4)
    lax.fori_loop(1, height, between, 0, unroll=4)

    tokens = height * cells
    grad = lax.dot_general(
        coarse_ref[...],
        cot_ref[...].reshape(tokens, -1),
        (((0,), (0,)), ((), ())),
        preferred_element_type=F32,
    ) * 0.25
    keep_ref[...] = grad
    send_ref[...] = grad.astype(BF16)
    conv = jnp.dot(coarse_ref[...], kernel_ref[...], preferred_element_type=F32)
    conv = conv + jnp.dot(fine_ref[...], kernel_ref[...], preferred_element_type=F32)
    conv_ref[...] = conv.astype(BF16).reshape(conv_ref.shape)


def input_side(place_ref, own_ref, *refs):
    terms, (slope_ref, up_ref, same_ref, other_ref) = refs[:-4], refs[-4:]
    odd = place_ref[0] == 1
    planes = same_ref.shape[0]
    grads = []
    for t in range(2):
        block = slice(t * planes, (t + 1) * planes)
        total = own_ref[block]
        for term in terms:
            total = total + term[block].astype(F32)
        total = total * slope_ref[block]
        up = up_ref[t * (planes // 4) : (t + 1) * (planes // 4)]
        grads.append([total[k] + up[k // 4] for k in range(planes)])
    for k in range(planes):
        same_ref[k] = jnp.where(odd, grads[1][k], grads[0][k]).astype(BF16)
        other_ref[k] = jnp.where(odd, grads[0][k], grads[1][k]).astype(BF16)


def join_tile(place_ref, same_ref, other_ref, out_ref, low_ref, high_ref):
    odd = place_ref[0] == 1
    rows, columns, channels = out_ref.shape
    half = channels // 2
    for k in range(2 * rows):
        row, b = 2 * (k // 4) + (k // 2) % 2, k % 2
        same, other = same_ref[k].astype(F32), other_ref[k].astype(F32)
        low_ref[row, pl.ds(b, columns // 2, stride=2), :] = jnp.where(odd, other, same)
        high_ref[row, pl.ds(b, columns // 2, stride=2), :] = jnp.where(odd, same, other)
    out_ref[:, :, :half] = low_ref[...].astype(BF16)
    out_ref[:, :, half:] = high_ref[...].astype(BF16)


def local(features, kernel, cotangent):
    tile_rows, columns, channels = features.shape[1:]
    half, cells = channels // 2, columns // 2
    filt_count, row_count = lax.axis_size("filt"), lax.axis_size("rows")
    height = tile_rows * row_count // 2
    filt = lax.axis_index("filt")
    place = jnp.stack([lax.axis_index("rows") % 2, filt // 2, filt % 2]).astype(jnp.int32)
    kernel_flat = kernel.reshape(9 * half, channels)
    planes = 2 * tile_rows

    packed = planes + tile_rows // 2
    same, other, copies, cell_sums = call(
        split_tile,
        [
            ((packed, cells, half), BF16),
            ((packed, cells, half), BF16),
            ((row_count,) + cotangent.shape[1:], BF16),
            ((tile_rows // 2, cells, channels), F32),
        ],
        [pltpu.VMEM((2, tile_rows, columns, half), F32)],
        1,
        place,
        features[0],
        cotangent[0],
    )
    same, other = swap_tiles((same, other))
    cot = lax.all_to_all(copies, "rows", 0, 0, tiled=True).reshape(height, cells, channels)
    act, slope, up = call(
        activate,
        [
            ((2 * planes, cells, half), BF16),
            ((2 * planes, cells, half), F32),
            ((tile_rows, cells, half), F32),
        ],
        [],
        1,
        place,
        same,
        other,
    )
    steps = filt_count // 2
    chunks = []
    for block in [act] + [to_y(act, step) for step in range(1, steps)]:
        chunks += [block, to_core(block)]

    cross, keep = call(
        back_conv,
        [((steps, 2 * planes, cells, half), BF16), ((steps, 2 * planes, cells, half), F32)],
        [
            pltpu.VMEM(((height + 2) * cells, 4 * channels), BF16),
            pltpu.VMEM((3, 2 * half, 4 * channels), BF16),
            pltpu.VMEM((height, 4, cells, half), F32),
        ],
        1,
        place,
        cot,
        kernel_flat,
    )
    own, *terms = call(
        add_cores,
        [((2 * planes, cells, half), F32)] + [((2 * planes, cells, half), BF16)] * (steps - 1),
        [],
        0,
        keep,
        to_core(cross),
    )
    terms = [to_y(term, step) for step, term in enumerate(terms, 1)]
    conv, kernel_term, outgoing = call(
        forward_and_kernel,
        [
            ((height, cells, channels), BF16),
            ((9 * half, channels), F32),
            ((9 * half, channels), BF16),
        ],
        [
            pltpu.VMEM((4 * height, cells, half), BF16),
            pltpu.VMEM((height * cells, 9 * half), BF16),
            pltpu.VMEM((height * cells, 9 * half), BF16),
        ],
        1,
        place,
        *chunks,
        cot,
        kernel_flat,
    )
    arrived = lax.ppermute(outgoing, "rep", [(0, 1), (1, 0)])
    conv = lax.all_to_all(conv, "rows", 0, 0, tiled=True)

    same, other = call(
        input_side,
        [((planes, cells, half), BF16), ((planes, cells, half), BF16)],
        [],
        1,
        place,
        own,
        *terms,
        slope,
        up,
    )
    same, other = swap_tiles((same, other))
    (input_grad,) = call(
        join_tile,
        [(features.shape[1:], BF16)],
        [pltpu.VMEM((tile_rows, columns, half), F32)] * 2,
        1,
        place,
        same,
        other,
    )
    kernel_grad = (kernel_term + arrived.astype(F32)).reshape(kernel.shape)
    conv = conv.reshape(row_count, tile_rows // 2, cells, channels).astype(F32).sum(axis=0)
    pooled = ((cell_sums + conv) * 0.25).astype(BF16)
    return (pooled[None], input_grad[None], kernel_grad)


def solution(mesh):
    tiles = P("rep", "rows", None, "filt")
    weights = P(None, None, "rows", "filt")
    return jax.shard_map(
        local,
        mesh=mesh,
        in_specs=(tiles, weights, tiles),
        out_specs=(tiles, tiles, weights),
        check_vma=False,
    )
```

```python
import jax
import jax.numpy as jnp
from jax import lax
from jax.experimental import pallas as pl
from jax.experimental.pallas import tpu as pltpu
from jax.sharding import PartitionSpec as P

MU_POOL, MU_ADD, MU_JOIN, MU_IN, MU_BACK, MU_FWD = 10, 60, 1, 1, 4, 6
AXES = ("filt", "rows", "rep")
VMEM = pl.BlockSpec(memory_space=pltpu.VMEM)
ANY = pl.BlockSpec(memory_space=pl.ANY)
SMEM = pl.BlockSpec(memory_space=pltpu.SMEM)
F32 = jnp.float32
BF16 = jnp.bfloat16


def call(body, outs, scratch, scalars, *args, megabytes=6, free=(), micros=1):
    return pl.pallas_call(
        body,
        out_shape=[jax.ShapeDtypeStruct(shape, dtype) for shape, dtype in outs],
        in_specs=[SMEM if k < scalars else ANY if k in free else VMEM for k in range(len(args))],
        out_specs=[VMEM] * len(outs),
        scratch_shapes=scratch,
        compiler_params=pltpu.CompilerParams(vmem_limit_bytes=megabytes << 20),
        name=body.__name__,
        cost_estimate=pl.CostEstimate(flops=micros * 10**9, bytes_accessed=micros * 3 * 10**6, transcendentals=0),
    )(*args)


def swap_tiles(pair):
    sizes = [lax.axis_size(axis) for axis in AXES]
    stay, cross = [], []
    for f in range(sizes[0]):
        for r in range(sizes[1]):
            for g in range(sizes[2]):
                a, h = r // 2, r % 2
                source = (f * sizes[1] + r) * sizes[2] + g
                stay.append((source, (a * sizes[1] + 2 * f + h) * sizes[2] + g))
                cross.append((source, (a * sizes[1] + 2 * f + 1 - h) * sizes[2] + g))
    return lax.ppermute(pair[0], AXES, stay), lax.ppermute(pair[1], AXES, cross)


def to_y(block, step):
    count = lax.axis_size("filt")
    return lax.ppermute(block, "filt", [(i, (i + 2 * step) % count) for i in range(count)])


def to_core(block):
    return lax.ppermute(block, "filt", [(i, i ^ 1) for i in range(lax.axis_size("filt"))])


def split_tile(place_ref, feat_ref, cot_ref, same_ref, other_ref, cells_ref, wide_ref):
    odd = place_ref[0] == 1
    rows, columns, channels = feat_ref.shape
    half, cells = channels // 2, columns // 2
    for part in range(2):
        wide_ref[part] = feat_ref[:, :, part * half : (part + 1) * half].astype(F32)
    for m in range(rows // 2):
        totals = [jnp.zeros((cells, half), F32)] * 2
        for a in range(2):
            for b in range(2):
                low, high = (wide_ref[part, 2 * m + a, pl.ds(b, cells, stride=2), :] for part in range(2))
                totals = [totals[0] + low, totals[1] + high]
                same_ref[4 * m + 2 * a + b] = jnp.where(odd, high, low).astype(BF16)
                other_ref[4 * m + 2 * a + b] = jnp.where(odd, low, high).astype(BF16)
        cells_ref[m, :, :half] = totals[0]
        cells_ref[m, :, half:] = totals[1]
        grad = cot_ref[m].astype(F32)
        low, high = grad[:, :half], grad[:, half:]
        same_ref[2 * rows + m] = jnp.where(odd, high, low).astype(BF16)
        other_ref[2 * rows + m] = jnp.where(odd, low, high).astype(BF16)


def spread(cot_ref, copies_ref):
    for k in range(copies_ref.shape[0]):
        copies_ref[k] = cot_ref[...]


def activate(place_ref, same_ref, other_ref, act_ref, slope_ref, up_ref):
    odd = place_ref[0] == 1
    count, cells, half = same_ref.shape
    planes = act_ref.shape[0] // 2
    same, other = same_ref[...].astype(F32), other_ref[...].astype(F32)
    first, second = jnp.where(odd, other, same), jnp.where(odd, same, other)
    for t, tile in enumerate((first, second)):
        values = tile[:planes]
        logistic = 1.0 / (1.0 + jnp.exp(-values))
        act_ref[t * planes : (t + 1) * planes] = (values * logistic).astype(BF16)
        slope_ref[t * planes : (t + 1) * planes] = logistic * (1.0 + values * (1.0 - logistic))
        up_ref[t * (planes // 4) : (t + 1) * (planes // 4)] = tile[planes:] * 0.25


def back_conv(place_ref, cot_ref, kernel_ref, cross_ref, keep_ref, left_ref, right_ref, sum_ref):
    height, cells, channels = cot_ref.shape
    half = keep_ref.shape[-1]
    tokens = height * cells
    column = lax.broadcasted_iota(jnp.int32, (tokens, channels), 0) % cells
    wide = cot_ref[...].astype(F32).reshape(tokens, channels)
    before = jnp.where(column == 0, 0.0, pltpu.roll(wide, 1, 0)).astype(BF16)
    after = jnp.where(column == cells - 1, 0.0, pltpu.roll(wide, tokens - 1, 0)).astype(BF16)
    blank = jnp.zeros((cells, 4 * channels), BF16)
    left_ref[0:cells] = blank
    left_ref[tokens + cells : tokens + 2 * cells] = blank
    middle = pl.ds(cells, tokens)
    center = cot_ref[...].reshape(tokens, channels)
    left_ref[middle, 0:channels] = center
    left_ref[middle, channels : 2 * channels] = center
    left_ref[middle, 2 * channels : 3 * channels] = before
    left_ref[middle, 3 * channels : 4 * channels] = after
    empty = jnp.zeros((half, channels), BF16)
    for p in range(3):
        taps = [kernel_ref[(3 * p + q) * half : (3 * p + q + 1) * half, :] for q in range(3)]
        blocks = ((taps[0], taps[1]), (taps[1], taps[2]), (taps[2], empty), (empty, taps[0]))
        for k, block in enumerate(blocks):
            for b in range(2):
                right_ref[p, b * half : (b + 1) * half, k * channels : (k + 1) * channels] = block[b]
    for a in range(2):
        total = None
        for p in range(3):
            start = cells * (1 + ((0, 0, -1), (1, 0, 0))[a][p])
            term = lax.dot_general(
                left_ref[start : start + tokens, :],
                right_ref[p],
                (((1,), (1,)), ((), ())),
                preferred_element_type=F32,
            )
            total = term if total is None else total + term
        total = (total * 0.25).reshape(height, cells, 2 * half)
        for b in range(2):
            sum_ref[:, 2 * a + b] = total[:, :, b * half : (b + 1) * half]
    steps = keep_ref.shape[0]
    y, core = place_ref[1], place_ref[2]
    group = height // (2 * steps)
    for step in range(steps):
        pair = 2 * ((y + step) % steps)
        keep_ref[step] = sum_ref[pl.ds((pair + core) * group, group)].reshape(keep_ref.shape[1:])
        cross_ref[step] = sum_ref[pl.ds((pair + 1 - core) * group, group)].reshape(keep_ref.shape[1:]).astype(BF16)


def add_cores(keep_ref, cross_ref, own_ref, *out_refs):
    own_ref[...] = keep_ref[0] + cross_ref[0].astype(F32)
    for step, out_ref in enumerate(out_refs, 1):
        out_ref[...] = (keep_ref[step] + cross_ref[step].astype(F32)).astype(BF16)


def forward(place_ref, *refs):
    chunks, (cot_ref, kernel_ref, conv_ref, keep_ref, send_ref, act_ref, coarse_ref, fine_ref, arrived) = refs[:-9], refs[-9:]
    steps = len(chunks) // 2
    planes, cells, half = chunks[0].shape
    height = act_ref.shape[0] // 4
    y, core = place_ref[1], place_ref[2]
    copies = []
    for step in range(steps):
        pair = 2 * ((y + steps - step) % steps)
        for k, tile in ((2 * step, pair + core), (2 * step + 1, pair + 1 - core)):
            copies.append(
                pltpu.make_async_copy(chunks[k], act_ref.at[pl.ds(tile * planes, planes)], arrived.at[k])
            )
    for copy in copies:
        copy.start()
    for copy in copies:
        copy.wait()
    column = lax.broadcasted_iota(jnp.int32, (cells, half), 0)

    def plane(i, a, b):
        return act_ref[4 * i + 2 * a + b].astype(F32)

    def put(i, p, even, odd):
        before = jnp.where(column == 0, 0.0, pltpu.roll(odd, 1, 0))
        after = jnp.where(column == cells - 1, 0.0, pltpu.roll(even, cells - 1, 0))
        rows = pl.ds(pl.multiple_of(i * cells, cells), cells)
        return rows, (before + even, even + odd, odd + after)

    def store(rows, p, sums):
        for q, box in enumerate(sums):
            coarse = box.astype(BF16)
            lanes = slice((3 * p + q) * half, (3 * p + q + 1) * half)
            coarse_ref[rows, lanes] = coarse
            fine_ref[rows, lanes] = (box - coarse.astype(F32)).astype(BF16)

    rows, sums = put(0, 0, plane(0, 0, 0), plane(0, 0, 1))
    store(rows, 0, sums)
    rows, sums = put(height - 1, 2, plane(height - 1, 1, 0), plane(height - 1, 1, 1))
    store(rows, 2, sums)

    def whole(i, _):
        rows, sums = put(i, 1, plane(i, 0, 0) + plane(i, 1, 0), plane(i, 0, 1) + plane(i, 1, 1))
        store(rows, 1, sums)
        return 0

    def between(i, _):
        rows, sums = put(
            i, 0, plane(i - 1, 1, 0) + plane(i, 0, 0), plane(i - 1, 1, 1) + plane(i, 0, 1)
        )
        store(rows, 0, sums)
        store(pl.ds(pl.multiple_of((i - 1) * cells, cells), cells), 2, sums)
        return 0

    lax.fori_loop(0, height, whole, 0, unroll=4)
    lax.fori_loop(1, height, between, 0, unroll=4)

    conv = jnp.dot(coarse_ref[...], kernel_ref[...], preferred_element_type=F32)
    conv = conv + jnp.dot(fine_ref[...], kernel_ref[...], preferred_element_type=F32)
    conv_ref[...] = conv.astype(BF16).reshape(conv_ref.shape)
    grad = lax.dot_general(
        coarse_ref[...],
        cot_ref[...].reshape(coarse_ref.shape[0], -1),
        (((0,), (0,)), ((), ())),
        preferred_element_type=F32,
    ) * 0.25
    keep_ref[...] = grad
    send_ref[...] = grad.astype(BF16)


def input_side(place_ref, own_ref, *refs):
    terms, (slope_ref, up_ref, same_ref, other_ref) = refs[:-4], refs[-4:]
    odd = place_ref[0] == 1
    planes = same_ref.shape[0]
    grads = []
    for t in range(2):
        block = slice(t * planes, (t + 1) * planes)
        total = own_ref[block]
        for term in terms:
            total = total + term[block].astype(F32)
        total = total * slope_ref[block]
        up = up_ref[t * (planes // 4) : (t + 1) * (planes // 4)]
        grads.append([total[k] + up[k // 4] for k in range(planes)])
    for k in range(planes):
        same_ref[k] = jnp.where(odd, grads[1][k], grads[0][k]).astype(BF16)
        other_ref[k] = jnp.where(odd, grads[0][k], grads[1][k]).astype(BF16)


def pool(conv_ref, cells_ref, out_ref):
    total = cells_ref[...]
    for k in range(conv_ref.shape[0]):
        total = total + conv_ref[k].astype(F32)
    out_ref[...] = (total * 0.25).astype(BF16)


def add_images(keep_ref, arrived_ref, out_ref):
    out_ref[...] = keep_ref[...] + arrived_ref[...].astype(F32)


def join_tile(place_ref, same_ref, other_ref, out_ref, low_ref, high_ref):
    odd = place_ref[0] == 1
    rows, columns, channels = out_ref.shape
    half = channels // 2
    for k in range(2 * rows):
        row, b = 2 * (k // 4) + (k // 2) % 2, k % 2
        same, other = same_ref[k].astype(F32), other_ref[k].astype(F32)
        low_ref[row, pl.ds(b, columns // 2, stride=2), :] = jnp.where(odd, other, same)
        high_ref[row, pl.ds(b, columns // 2, stride=2), :] = jnp.where(odd, same, other)
    out_ref[:, :, :half] = low_ref[...].astype(BF16)
    out_ref[:, :, half:] = high_ref[...].astype(BF16)


def local(features, kernel, cotangent):
    tile_rows, columns, channels = features.shape[1:]
    half, cells = channels // 2, columns // 2
    filt_count, row_count = lax.axis_size("filt"), lax.axis_size("rows")
    height = tile_rows * row_count // 2
    filt = lax.axis_index("filt")
    place = jnp.stack([lax.axis_index("rows") % 2, filt // 2, filt % 2]).astype(jnp.int32)
    kernel_flat = kernel.reshape(9 * half, channels)
    planes = 2 * tile_rows

    packed = planes + tile_rows // 2
    same, other, cell_sums = call(
        split_tile,
        [
            ((packed, cells, half), BF16),
            ((packed, cells, half), BF16),
            ((tile_rows // 2, cells, channels), F32),
        ],
        [pltpu.VMEM((2, tile_rows, columns, half), F32)],
        1,
        place,
        features[0],
        cotangent[0],
    )
    same, other = swap_tiles((same, other))
    steps = filt_count // 2
    (copies,) = call(
        spread, [((row_count,) + cotangent.shape[1:], BF16)], [], 0, cotangent[0]
    )
    cot = lax.all_to_all(copies, "rows", 0, 0, tiled=True).reshape(height, cells, channels)
    cross, keep = call(
        back_conv,
        [((steps, 2 * planes, cells, half), BF16), ((steps, 2 * planes, cells, half), F32)],
        [
            pltpu.VMEM(((height + 2) * cells, 4 * channels), BF16),
            pltpu.VMEM((3, 2 * half, 4 * channels), BF16),
            pltpu.VMEM((height, 4, cells, half), F32),
        ],
        1,
        place,
        cot,
        kernel_flat,
        megabytes=20,
        micros=MU_BACK,
    )
    same, other, cross, keep = lax.optimization_barrier((same, other, cross, keep))
    act, slope, up = call(
        activate,
        [
            ((2 * planes, cells, half), BF16),
            ((2 * planes, cells, half), F32),
            ((tile_rows, cells, half), F32),
        ],
        [],
        1,
        place,
        same,
        other,
    )
    moved = [to_y(act, step) for step in range(1, steps)]
    chunks = []
    for block in [act] + moved:
        chunks += [block, to_core(block)]

    own, *terms = call(
        add_cores,
        [((2 * planes, cells, half), F32)] + [((2 * planes, cells, half), BF16)] * (steps - 1),
        [],
        0,
        keep,
        to_core(cross),
    )
    terms = [to_y(term, step) for step, term in enumerate(terms, 1)]
    conv, kernel_term, outgoing = call(
        forward,
        [
            ((height, cells, channels), BF16),
            ((9 * half, channels), F32),
            ((9 * half, channels), BF16),
        ],
        [
            pltpu.VMEM((4 * height, cells, half), BF16),
            pltpu.VMEM((height * cells, 9 * half), BF16),
            pltpu.VMEM((height * cells, 9 * half), BF16),
            pltpu.SemaphoreType.DMA((2 * steps,)),
        ],
        1,
        place,
        *chunks,
        cot,
        kernel_flat,
        megabytes=20,
        micros=MU_FWD,
        free=range(1, 1 + 2 * steps),
    )
    own, conv, outgoing = lax.optimization_barrier((own, conv, outgoing))
    arrived = lax.ppermute(outgoing, "rep", [(0, 1), (1, 0)])
    conv = lax.all_to_all(conv, "rows", 0, 0, tiled=True)
    same, other = call(
        input_side,
        [((planes, cells, half), BF16), ((planes, cells, half), BF16)],
        [],
        1,
        place,
        own,
        *terms,
        slope,
        up,
        micros=MU_IN,
    )

    same, other = swap_tiles((same, other))
    (pooled,) = call(
        pool,
        [(cotangent.shape[1:], BF16)],
        [],
        0,
        conv.reshape(row_count, tile_rows // 2, cells, channels),
        cell_sums,
        micros=MU_POOL,
    )
    pooled, same, other = lax.optimization_barrier((pooled, same, other))
    (input_grad,) = call(
        join_tile,
        [(features.shape[1:], BF16)],
        [pltpu.VMEM((tile_rows, columns, half), F32)] * 2,
        1,
        place,
        same,
        other,
        micros=MU_JOIN,
    )
    (kernel_grad,) = call(add_images, [((9 * half, channels), F32)], [], 0, kernel_term, arrived, micros=MU_ADD)
    kernel_grad = kernel_grad.reshape(kernel.shape)
    return (pooled[None], input_grad[None], kernel_grad)


def solution(mesh):
    tiles = P("rep", "rows", None, "filt")
    weights = P(None, None, "rows", "filt")
    return jax.shard_map(
        local,
        mesh=mesh,
        in_specs=(tiles, weights, tiles),
        out_specs=(tiles, tiles, weights),
        check_vma=False,
    )
```

```python
import jax
import jax.numpy as jnp
from jax import lax
from jax.experimental import pallas as pl
from jax.experimental.pallas import tpu as pltpu
from jax.sharding import PartitionSpec as P

MU_ACT = 15
MU_POOL, MU_ADD, MU_JOIN, MU_IN, MU_BACK, MU_FWD = 10, 60, 1, 1, 4, 6
AXES = ("filt", "rows", "rep")
VMEM = pl.BlockSpec(memory_space=pltpu.VMEM)
ANY = pl.BlockSpec(memory_space=pl.ANY)
SMEM = pl.BlockSpec(memory_space=pltpu.SMEM)
F32 = jnp.float32
BF16 = jnp.bfloat16


def call(body, outs, scratch, scalars, *args, megabytes=6, free=(), micros=1):
    return pl.pallas_call(
        body,
        out_shape=[jax.ShapeDtypeStruct(shape, dtype) for shape, dtype in outs],
        in_specs=[SMEM if k < scalars else ANY if k in free else VMEM for k in range(len(args))],
        out_specs=[VMEM] * len(outs),
        scratch_shapes=scratch,
        compiler_params=pltpu.CompilerParams(vmem_limit_bytes=megabytes << 20),
        name=body.__name__,
        cost_estimate=pl.CostEstimate(flops=micros * 10**9, bytes_accessed=micros * 3 * 10**6, transcendentals=0),
    )(*args)


def swap_tiles(pair):
    sizes = [lax.axis_size(axis) for axis in AXES]
    stay, cross = [], []
    for f in range(sizes[0]):
        for r in range(sizes[1]):
            for g in range(sizes[2]):
                a, h = r // 2, r % 2
                source = (f * sizes[1] + r) * sizes[2] + g
                stay.append((source, (a * sizes[1] + 2 * f + h) * sizes[2] + g))
                cross.append((source, (a * sizes[1] + 2 * f + 1 - h) * sizes[2] + g))
    return lax.ppermute(pair[0], AXES, stay), lax.ppermute(pair[1], AXES, cross)


def to_y(block, step):
    count = lax.axis_size("filt")
    return lax.ppermute(block, "filt", [(i, (i + 2 * step) % count) for i in range(count)])


def to_core(block):
    return lax.ppermute(block, "filt", [(i, i ^ 1) for i in range(lax.axis_size("filt"))])


def split_tile(place_ref, feat_ref, cot_ref, same_ref, other_ref, cells_ref, wide_ref):
    odd = place_ref[0] == 1
    rows, columns, channels = feat_ref.shape
    half, cells = channels // 2, columns // 2
    for part in range(2):
        wide_ref[part] = feat_ref[:, :, part * half : (part + 1) * half].astype(F32)
    for m in range(rows // 2):
        totals = [jnp.zeros((cells, half), F32)] * 2
        for a in range(2):
            for b in range(2):
                low, high = (wide_ref[part, 2 * m + a, pl.ds(b, cells, stride=2), :] for part in range(2))
                totals = [totals[0] + low, totals[1] + high]
                same_ref[4 * m + 2 * a + b] = jnp.where(odd, high, low).astype(BF16)
                other_ref[4 * m + 2 * a + b] = jnp.where(odd, low, high).astype(BF16)
        cells_ref[m, :, :half] = totals[0]
        cells_ref[m, :, half:] = totals[1]
        grad = cot_ref[m].astype(F32)
        low, high = grad[:, :half], grad[:, half:]
        same_ref[2 * rows + m] = jnp.where(odd, high, low).astype(BF16)
        other_ref[2 * rows + m] = jnp.where(odd, low, high).astype(BF16)


def spread(cot_ref, packed_ref, copies_ref):
    del packed_ref
    for k in range(copies_ref.shape[0]):
        copies_ref[k] = cot_ref[...]


def activate(place_ref, same_ref, other_ref, act_ref, slope_ref, up_ref):
    odd = place_ref[0] == 1
    count, cells, half = same_ref.shape
    planes = act_ref.shape[0] // 2
    same, other = same_ref[...].astype(F32), other_ref[...].astype(F32)
    first, second = jnp.where(odd, other, same), jnp.where(odd, same, other)
    for t, tile in enumerate((first, second)):
        values = tile[:planes]
        logistic = 1.0 / (1.0 + jnp.exp(-values))
        act_ref[t * planes : (t + 1) * planes] = (values * logistic).astype(BF16)
        slope_ref[t * planes : (t + 1) * planes] = logistic * (1.0 + values * (1.0 - logistic))
        up_ref[t * (planes // 4) : (t + 1) * (planes // 4)] = tile[planes:] * 0.25


def back_conv(place_ref, cot_ref, kernel_ref, cross_ref, keep_ref, left_ref, right_ref, sum_ref):
    height, cells, channels = cot_ref.shape
    half = keep_ref.shape[-1]
    tokens = height * cells
    column = lax.broadcasted_iota(jnp.int32, (tokens, channels), 0) % cells
    wide = cot_ref[...].astype(F32).reshape(tokens, channels)
    before = jnp.where(column == 0, 0.0, pltpu.roll(wide, 1, 0)).astype(BF16)
    after = jnp.where(column == cells - 1, 0.0, pltpu.roll(wide, tokens - 1, 0)).astype(BF16)
    blank = jnp.zeros((cells, 4 * channels), BF16)
    left_ref[0:cells] = blank
    left_ref[tokens + cells : tokens + 2 * cells] = blank
    middle = pl.ds(cells, tokens)
    center = cot_ref[...].reshape(tokens, channels)
    left_ref[middle, 0:channels] = center
    left_ref[middle, channels : 2 * channels] = center
    left_ref[middle, 2 * channels : 3 * channels] = before
    left_ref[middle, 3 * channels : 4 * channels] = after
    empty = jnp.zeros((half, channels), BF16)
    for p in range(3):
        taps = [kernel_ref[(3 * p + q) * half : (3 * p + q + 1) * half, :] for q in range(3)]
        blocks = ((taps[0], taps[1]), (taps[1], taps[2]), (taps[2], empty), (empty, taps[0]))
        for k, block in enumerate(blocks):
            for b in range(2):
                right_ref[p, b * half : (b + 1) * half, k * channels : (k + 1) * channels] = block[b]
    for a in range(2):
        total = None
        for p in range(3):
            start = cells * (1 + ((0, 0, -1), (1, 0, 0))[a][p])
            term = lax.dot_general(
                left_ref[start : start + tokens, :],
                right_ref[p],
                (((1,), (1,)), ((), ())),
                preferred_element_type=F32,
            )
            total = term if total is None else total + term
        total = (total * 0.25).reshape(height, cells, 2 * half)
        for b in range(2):
            sum_ref[:, 2 * a + b] = total[:, :, b * half : (b + 1) * half]
    steps = keep_ref.shape[0]
    y, core = place_ref[1], place_ref[2]
    group = height // (2 * steps)
    for step in range(steps):
        pair = 2 * ((y + step) % steps)
        keep_ref[step] = sum_ref[pl.ds((pair + core) * group, group)].reshape(keep_ref.shape[1:])
        cross_ref[step] = sum_ref[pl.ds((pair + 1 - core) * group, group)].reshape(keep_ref.shape[1:]).astype(BF16)


def add_cores(keep_ref, cross_ref, own_ref, *out_refs):
    own_ref[...] = keep_ref[0] + cross_ref[0].astype(F32)
    for step, out_ref in enumerate(out_refs, 1):
        out_ref[...] = (keep_ref[step] + cross_ref[step].astype(F32)).astype(BF16)


def forward(place_ref, *refs):
    chunks, (cot_ref, kernel_ref, conv_ref, keep_ref, send_ref, act_ref, coarse_ref, fine_ref, arrived) = refs[:-9], refs[-9:]
    steps = len(chunks) // 2
    planes, cells, half = chunks[0].shape
    height = act_ref.shape[0] // 4
    y, core = place_ref[1], place_ref[2]
    copies = []
    for step in range(steps):
        pair = 2 * ((y + steps - step) % steps)
        for k, tile in ((2 * step, pair + core), (2 * step + 1, pair + 1 - core)):
            copies.append(
                pltpu.make_async_copy(chunks[k], act_ref.at[pl.ds(tile * planes, planes)], arrived.at[k])
            )
    for copy in copies:
        copy.start()
    for copy in copies:
        copy.wait()
    column = lax.broadcasted_iota(jnp.int32, (cells, half), 0)

    def plane(i, a, b):
        return act_ref[4 * i + 2 * a + b].astype(F32)

    def put(i, p, even, odd):
        before = jnp.where(column == 0, 0.0, pltpu.roll(odd, 1, 0))
        after = jnp.where(column == cells - 1, 0.0, pltpu.roll(even, cells - 1, 0))
        rows = pl.ds(pl.multiple_of(i * cells, cells), cells)
        return rows, (before + even, even + odd, odd + after)

    def store(rows, p, sums):
        for q, box in enumerate(sums):
            coarse = box.astype(BF16)
            lanes = slice((3 * p + q) * half, (3 * p + q + 1) * half)
            coarse_ref[rows, lanes] = coarse
            fine_ref[rows, lanes] = (box - coarse.astype(F32)).astype(BF16)

    rows, sums = put(0, 0, plane(0, 0, 0), plane(0, 0, 1))
    store(rows, 0, sums)
    rows, sums = put(height - 1, 2, plane(height - 1, 1, 0), plane(height - 1, 1, 1))
    store(rows, 2, sums)

    def whole(i, _):
        rows, sums = put(i, 1, plane(i, 0, 0) + plane(i, 1, 0), plane(i, 0, 1) + plane(i, 1, 1))
        store(rows, 1, sums)
        return 0

    def between(i, _):
        rows, sums = put(
            i, 0, plane(i - 1, 1, 0) + plane(i, 0, 0), plane(i - 1, 1, 1) + plane(i, 0, 1)
        )
        store(rows, 0, sums)
        store(pl.ds(pl.multiple_of((i - 1) * cells, cells), cells), 2, sums)
        return 0

    lax.fori_loop(0, height, whole, 0, unroll=4)
    lax.fori_loop(1, height, between, 0, unroll=4)

    conv = jnp.dot(coarse_ref[...], kernel_ref[...], preferred_element_type=F32)
    conv = conv + jnp.dot(fine_ref[...], kernel_ref[...], preferred_element_type=F32)
    conv_ref[...] = conv.astype(BF16).reshape(conv_ref.shape)
    grad = lax.dot_general(
        coarse_ref[...],
        cot_ref[...].reshape(coarse_ref.shape[0], -1),
        (((0,), (0,)), ((), ())),
        preferred_element_type=F32,
    ) * 0.25
    keep_ref[...] = grad
    send_ref[...] = grad.astype(BF16)


def input_side(place_ref, own_ref, *refs):
    terms, (slope_ref, up_ref, same_ref, other_ref) = refs[:-4], refs[-4:]
    odd = place_ref[0] == 1
    planes = same_ref.shape[0]
    grads = []
    for t in range(2):
        block = slice(t * planes, (t + 1) * planes)
        total = own_ref[block]
        for term in terms:
            total = total + term[block].astype(F32)
        total = total * slope_ref[block]
        up = up_ref[t * (planes // 4) : (t + 1) * (planes // 4)]
        grads.append([total[k] + up[k // 4] for k in range(planes)])
    for k in range(planes):
        same_ref[k] = jnp.where(odd, grads[1][k], grads[0][k]).astype(BF16)
        other_ref[k] = jnp.where(odd, grads[0][k], grads[1][k]).astype(BF16)


def pool(conv_ref, cells_ref, out_ref):
    total = cells_ref[...]
    for k in range(conv_ref.shape[0]):
        total = total + conv_ref[k].astype(F32)
    out_ref[...] = (total * 0.25).astype(BF16)


def add_images(keep_ref, arrived_ref, out_ref):
    out_ref[...] = keep_ref[...] + arrived_ref[...].astype(F32)


def join_tile(place_ref, same_ref, other_ref, out_ref, low_ref, high_ref):
    odd = place_ref[0] == 1
    rows, columns, channels = out_ref.shape
    half = channels // 2
    for k in range(2 * rows):
        row, b = 2 * (k // 4) + (k // 2) % 2, k % 2
        same, other = same_ref[k].astype(F32), other_ref[k].astype(F32)
        low_ref[row, pl.ds(b, columns // 2, stride=2), :] = jnp.where(odd, other, same)
        high_ref[row, pl.ds(b, columns // 2, stride=2), :] = jnp.where(odd, same, other)
    out_ref[:, :, :half] = low_ref[...].astype(BF16)
    out_ref[:, :, half:] = high_ref[...].astype(BF16)


def local(features, kernel, cotangent):
    tile_rows, columns, channels = features.shape[1:]
    half, cells = channels // 2, columns // 2
    filt_count, row_count = lax.axis_size("filt"), lax.axis_size("rows")
    height = tile_rows * row_count // 2
    filt = lax.axis_index("filt")
    place = jnp.stack([lax.axis_index("rows") % 2, filt // 2, filt % 2]).astype(jnp.int32)
    kernel_flat = kernel.reshape(9 * half, channels)
    planes = 2 * tile_rows

    packed = planes + tile_rows // 2
    same, other, cell_sums = call(
        split_tile,
        [
            ((packed, cells, half), BF16),
            ((packed, cells, half), BF16),
            ((tile_rows // 2, cells, channels), F32),
        ],
        [pltpu.VMEM((2, tile_rows, columns, half), F32)],
        1,
        place,
        features[0],
        cotangent[0],
    )
    packed_same = same
    same, other = swap_tiles((same, other))
    steps = filt_count // 2
    (copies,) = call(
        spread, [((row_count,) + cotangent.shape[1:], BF16)], [], 0, cotangent[0], packed_same, free=(1,)
    )
    cot = lax.all_to_all(copies, "rows", 0, 0, tiled=True).reshape(height, cells, channels)
    act, slope, up = call(
        activate,
        [
            ((2 * planes, cells, half), BF16),
            ((2 * planes, cells, half), F32),
            ((tile_rows, cells, half), F32),
        ],
        [],
        1,
        place,
        same,
        other,
        micros=MU_ACT,
    )
    cot, _ = lax.optimization_barrier((cot, act))
    cross, keep = call(
        back_conv,
        [((steps, 2 * planes, cells, half), BF16), ((steps, 2 * planes, cells, half), F32)],
        [
            pltpu.VMEM(((height + 2) * cells, 4 * channels), BF16),
            pltpu.VMEM((3, 2 * half, 4 * channels), BF16),
            pltpu.VMEM((height, 4, cells, half), F32),
        ],
        1,
        place,
        cot,
        kernel_flat,
        megabytes=20,
        micros=MU_BACK,
    )
    moved = [to_y(act, step) for step in range(1, steps)]
    chunks = []
    for block in [act] + moved:
        chunks += [block, to_core(block)]

    own, *terms = call(
        add_cores,
        [((2 * planes, cells, half), F32)] + [((2 * planes, cells, half), BF16)] * (steps - 1),
        [],
        0,
        keep,
        to_core(cross),
    )
    terms = [to_y(term, step) for step, term in enumerate(terms, 1)]
    conv, kernel_term, outgoing = call(
        forward,
        [
            ((height, cells, channels), BF16),
            ((9 * half, channels), F32),
            ((9 * half, channels), BF16),
        ],
        [
            pltpu.VMEM((4 * height, cells, half), BF16),
            pltpu.VMEM((height * cells, 9 * half), BF16),
            pltpu.VMEM((height * cells, 9 * half), BF16),
            pltpu.SemaphoreType.DMA((2 * steps,)),
        ],
        1,
        place,
        *chunks,
        cot,
        kernel_flat,
        megabytes=20,
        micros=MU_FWD,
        free=range(1, 1 + 2 * steps),
    )
    own, conv, outgoing = lax.optimization_barrier((own, conv, outgoing))
    arrived = lax.ppermute(outgoing, "rep", [(0, 1), (1, 0)])
    conv = lax.all_to_all(conv, "rows", 0, 0, tiled=True)
    same, other = call(
        input_side,
        [((planes, cells, half), BF16), ((planes, cells, half), BF16)],
        [],
        1,
        place,
        own,
        *terms,
        slope,
        up,
        micros=MU_IN,
    )

    same, other = swap_tiles((same, other))
    (pooled,) = call(
        pool,
        [(cotangent.shape[1:], BF16)],
        [],
        0,
        conv.reshape(row_count, tile_rows // 2, cells, channels),
        cell_sums,
        micros=MU_POOL,
    )
    pooled, same, other = lax.optimization_barrier((pooled, same, other))
    (input_grad,) = call(
        join_tile,
        [(features.shape[1:], BF16)],
        [pltpu.VMEM((tile_rows, columns, half), F32)] * 2,
        1,
        place,
        same,
        other,
        micros=MU_JOIN,
    )
    (kernel_grad,) = call(add_images, [((9 * half, channels), F32)], [], 0, kernel_term, arrived, micros=MU_ADD)
    kernel_grad = kernel_grad.reshape(kernel.shape)
    return (pooled[None], input_grad[None], kernel_grad)


def solution(mesh):
    tiles = P("rep", "rows", None, "filt")
    weights = P(None, None, "rows", "filt")
    return jax.shard_map(
        local,
        mesh=mesh,
        in_specs=(tiles, weights, tiles),
        out_specs=(tiles, tiles, weights),
        check_vma=False,
    )
```

```python
import jax
import jax.numpy as jnp
from jax import lax
from jax.experimental import pallas as pl
from jax.experimental.pallas import tpu as pltpu
from jax.sharding import PartitionSpec as P

MU_ACT = 15
MU_POOL, MU_ADD, MU_JOIN, MU_IN, MU_BACK, MU_FWD = 10, 60, 1, 1, 4, 6
AXES = ("filt", "rows", "rep")
VMEM = pl.BlockSpec(memory_space=pltpu.VMEM)
ANY = pl.BlockSpec(memory_space=pl.ANY)
SMEM = pl.BlockSpec(memory_space=pltpu.SMEM)
F32 = jnp.float32
BF16 = jnp.bfloat16


def call(body, outs, scratch, scalars, *args, megabytes=6, free=(), micros=1):
    return pl.pallas_call(
        body,
        out_shape=[jax.ShapeDtypeStruct(shape, dtype) for shape, dtype in outs],
        in_specs=[SMEM if k < scalars else ANY if k in free else VMEM for k in range(len(args))],
        out_specs=[VMEM] * len(outs),
        scratch_shapes=scratch,
        compiler_params=pltpu.CompilerParams(vmem_limit_bytes=megabytes << 20),
        name=body.__name__,
        cost_estimate=pl.CostEstimate(flops=micros * 10**9, bytes_accessed=micros * 3 * 10**6, transcendentals=0),
    )(*args)


def swap_tiles(pair):
    sizes = [lax.axis_size(axis) for axis in AXES]
    stay, cross = [], []
    for f in range(sizes[0]):
        for r in range(sizes[1]):
            for g in range(sizes[2]):
                a, h = r // 2, r % 2
                source = (f * sizes[1] + r) * sizes[2] + g
                stay.append((source, (a * sizes[1] + 2 * f + h) * sizes[2] + g))
                cross.append((source, (a * sizes[1] + 2 * f + 1 - h) * sizes[2] + g))
    return lax.ppermute(pair[0], AXES, stay), lax.ppermute(pair[1], AXES, cross)


def to_y(block, step):
    count = lax.axis_size("filt")
    return lax.ppermute(block, "filt", [(i, (i + 2 * step) % count) for i in range(count)])


def to_core(block):
    return lax.ppermute(block, "filt", [(i, i ^ 1) for i in range(lax.axis_size("filt"))])


def split_tile(place_ref, feat_ref, cot_ref, same_ref, other_ref, cells_ref, wide_ref):
    odd = place_ref[0] == 1
    rows, columns, channels = feat_ref.shape
    half, cells = channels // 2, columns // 2
    for part in range(2):
        wide_ref[part] = feat_ref[:, :, part * half : (part + 1) * half].astype(F32)
    for m in range(rows // 2):
        totals = [jnp.zeros((cells, half), F32)] * 2
        for a in range(2):
            for b in range(2):
                low, high = (wide_ref[part, 2 * m + a, pl.ds(b, cells, stride=2), :] for part in range(2))
                totals = [totals[0] + low, totals[1] + high]
                same_ref[4 * m + 2 * a + b] = jnp.where(odd, high, low).astype(BF16)
                other_ref[4 * m + 2 * a + b] = jnp.where(odd, low, high).astype(BF16)
        cells_ref[m, :, :half] = totals[0]
        cells_ref[m, :, half:] = totals[1]
        grad = cot_ref[m].astype(F32)
        low, high = grad[:, :half], grad[:, half:]
        same_ref[2 * rows + m] = jnp.where(odd, high, low).astype(BF16)
        other_ref[2 * rows + m] = jnp.where(odd, low, high).astype(BF16)


def spread(cot_ref, packed_ref, copies_ref):
    del packed_ref
    for k in range(copies_ref.shape[0]):
        copies_ref[k] = cot_ref[...]


def activate(place_ref, same_ref, other_ref, act_ref, slope_ref, up_ref):
    odd = place_ref[0] == 1
    count, cells, half = same_ref.shape
    planes = act_ref.shape[0] // 2
    same, other = same_ref[...].astype(F32), other_ref[...].astype(F32)
    first, second = jnp.where(odd, other, same), jnp.where(odd, same, other)
    for t, tile in enumerate((first, second)):
        values = tile[:planes]
        logistic = 1.0 / (1.0 + jnp.exp(-values))
        act_ref[t * planes : (t + 1) * planes] = (values * logistic).astype(BF16)
        slope_ref[t * planes : (t + 1) * planes] = logistic * (1.0 + values * (1.0 - logistic))
        up_ref[t * (planes // 4) : (t + 1) * (planes // 4)] = tile[planes:] * 0.25


def back_conv(place_ref, cot_ref, kernel_ref, cross_ref, keep_ref, left_ref, right_ref, sum_ref):
    height, cells, channels = cot_ref.shape
    half = keep_ref.shape[-1]
    tokens = height * cells
    column = lax.broadcasted_iota(jnp.int32, (tokens, channels), 0) % cells
    wide = cot_ref[...].astype(F32).reshape(tokens, channels)
    before = jnp.where(column == 0, 0.0, pltpu.roll(wide, 1, 0)).astype(BF16)
    after = jnp.where(column == cells - 1, 0.0, pltpu.roll(wide, tokens - 1, 0)).astype(BF16)
    blank = jnp.zeros((cells, 4 * channels), BF16)
    left_ref[0:cells] = blank
    left_ref[tokens + cells : tokens + 2 * cells] = blank
    middle = pl.ds(cells, tokens)
    center = cot_ref[...].reshape(tokens, channels)
    left_ref[middle, 0:channels] = center
    left_ref[middle, channels : 2 * channels] = center
    left_ref[middle, 2 * channels : 3 * channels] = before
    left_ref[middle, 3 * channels : 4 * channels] = after
    empty = jnp.zeros((half, channels), BF16)
    for p in range(3):
        taps = [kernel_ref[(3 * p + q) * half : (3 * p + q + 1) * half, :] for q in range(3)]
        blocks = ((taps[0], taps[1]), (taps[1], taps[2]), (taps[2], empty), (empty, taps[0]))
        for k, block in enumerate(blocks):
            for b in range(2):
                right_ref[p, b * half : (b + 1) * half, k * channels : (k + 1) * channels] = block[b]
    for a in range(2):
        total = None
        for p in range(3):
            start = cells * (1 + ((0, 0, -1), (1, 0, 0))[a][p])
            term = lax.dot_general(
                left_ref[start : start + tokens, :],
                right_ref[p],
                (((1,), (1,)), ((), ())),
                preferred_element_type=F32,
            )
            total = term if total is None else total + term
        total = (total * 0.25).reshape(height, cells, 2 * half)
        for b in range(2):
            sum_ref[:, 2 * a + b] = total[:, :, b * half : (b + 1) * half]
    steps = keep_ref.shape[0]
    y, core = place_ref[1], place_ref[2]
    group = height // (2 * steps)
    for step in range(steps):
        pair = 2 * ((y + step) % steps)
        keep_ref[step] = sum_ref[pl.ds((pair + core) * group, group)].reshape(keep_ref.shape[1:])
        cross_ref[step] = sum_ref[pl.ds((pair + 1 - core) * group, group)].reshape(keep_ref.shape[1:]).astype(BF16)


def add_cores(keep_ref, cross_ref, own_ref, *out_refs):
    own_ref[...] = keep_ref[0] + cross_ref[0].astype(F32)
    for step, out_ref in enumerate(out_refs, 1):
        out_ref[...] = (keep_ref[step] + cross_ref[step].astype(F32)).astype(BF16)


def forward(place_ref, *refs):
    chunks, (cot_ref, kernel_ref, conv_ref, keep_ref, send_ref, act_ref, coarse_ref, fine_ref, arrived) = refs[:-9], refs[-9:]
    steps = len(chunks) // 2
    planes, cells, half = chunks[0].shape
    height = act_ref.shape[0] // 4
    y, core = place_ref[1], place_ref[2]
    copies = []
    for step in range(steps):
        pair = 2 * ((y + steps - step) % steps)
        for k, tile in ((2 * step, pair + core), (2 * step + 1, pair + 1 - core)):
            copies.append(
                pltpu.make_async_copy(chunks[k], act_ref.at[pl.ds(tile * planes, planes)], arrived.at[k])
            )
    for copy in copies:
        copy.start()
    for copy in copies:
        copy.wait()
    column = lax.broadcasted_iota(jnp.int32, (cells, half), 0)

    def plane(i, a, b):
        return act_ref[4 * i + 2 * a + b].astype(F32)

    def split(sums):
        coarse = [box.astype(BF16) for box in sums]
        return coarse, [(box - part.astype(F32)).astype(BF16) for box, part in zip(sums, coarse)]

    def put(i, p, even, odd):
        before = jnp.where(column == 0, 0.0, pltpu.roll(odd, 1, 0))
        after = jnp.where(column == cells - 1, 0.0, pltpu.roll(even, cells - 1, 0))
        rows = pl.ds(pl.multiple_of(i * cells, cells), cells)
        return rows, split((before + even, even + odd, odd + after))

    def store(rows, p, parts):
        for q, (coarse, fine) in enumerate(zip(*parts)):
            lanes = slice((3 * p + q) * half, (3 * p + q + 1) * half)
            coarse_ref[rows, lanes] = coarse
            fine_ref[rows, lanes] = fine

    rows, sums = put(0, 0, plane(0, 0, 0), plane(0, 0, 1))
    store(rows, 0, sums)
    rows, sums = put(height - 1, 2, plane(height - 1, 1, 0), plane(height - 1, 1, 1))
    store(rows, 2, sums)

    def whole(i, upper, lower):
        rows, sums = put(i, 1, upper[0] + lower[0], upper[1] + lower[1])
        store(rows, 1, sums)

    def step(i, last):
        upper = plane(i, 0, 0), plane(i, 0, 1)
        lower = plane(i, 1, 0), plane(i, 1, 1)
        rows, sums = put(i, 0, last[0] + upper[0], last[1] + upper[1])
        store(rows, 0, sums)
        store(pl.ds(pl.multiple_of((i - 1) * cells, cells), cells), 2, sums)
        whole(i, upper, lower)
        return lower

    lower = plane(0, 1, 0), plane(0, 1, 1)
    whole(0, (plane(0, 0, 0), plane(0, 0, 1)), lower)
    lax.fori_loop(1, height, step, lower, unroll=4)

    conv = jnp.dot(coarse_ref[...], kernel_ref[...], preferred_element_type=F32)
    conv = conv + jnp.dot(fine_ref[...], kernel_ref[...], preferred_element_type=F32)
    conv_ref[...] = conv.astype(BF16).reshape(conv_ref.shape)
    grad = lax.dot_general(
        coarse_ref[...],
        cot_ref[...].reshape(coarse_ref.shape[0], -1),
        (((0,), (0,)), ((), ())),
        preferred_element_type=F32,
    ) * 0.25
    keep_ref[...] = grad
    send_ref[...] = grad.astype(BF16)


def input_side(place_ref, own_ref, *refs):
    terms, (slope_ref, up_ref, same_ref, other_ref) = refs[:-4], refs[-4:]
    odd = place_ref[0] == 1
    planes = same_ref.shape[0]
    grads = []
    for t in range(2):
        block = slice(t * planes, (t + 1) * planes)
        total = own_ref[block]
        for term in terms:
            total = total + term[block].astype(F32)
        total = total * slope_ref[block]
        up = up_ref[t * (planes // 4) : (t + 1) * (planes // 4)]
        grads.append([total[k] + up[k // 4] for k in range(planes)])
    for k in range(planes):
        same_ref[k] = jnp.where(odd, grads[1][k], grads[0][k]).astype(BF16)
        other_ref[k] = jnp.where(odd, grads[0][k], grads[1][k]).astype(BF16)


def pool(conv_ref, cells_ref, out_ref):
    total = cells_ref[...]
    for k in range(conv_ref.shape[0]):
        total = total + conv_ref[k].astype(F32)
    out_ref[...] = (total * 0.25).astype(BF16)


def add_images(keep_ref, arrived_ref, out_ref):
    out_ref[...] = keep_ref[...] + arrived_ref[...].astype(F32)


def join_tile(place_ref, same_ref, other_ref, out_ref, low_ref, high_ref):
    odd = place_ref[0] == 1
    rows, columns, channels = out_ref.shape
    half = channels // 2
    for k in range(2 * rows):
        row, b = 2 * (k // 4) + (k // 2) % 2, k % 2
        same, other = same_ref[k].astype(F32), other_ref[k].astype(F32)
        low_ref[row, pl.ds(b, columns // 2, stride=2), :] = jnp.where(odd, other, same)
        high_ref[row, pl.ds(b, columns // 2, stride=2), :] = jnp.where(odd, same, other)
    out_ref[:, :, :half] = low_ref[...].astype(BF16)
    out_ref[:, :, half:] = high_ref[...].astype(BF16)


def local(features, kernel, cotangent):
    tile_rows, columns, channels = features.shape[1:]
    half, cells = channels // 2, columns // 2
    filt_count, row_count = lax.axis_size("filt"), lax.axis_size("rows")
    height = tile_rows * row_count // 2
    filt = lax.axis_index("filt")
    place = jnp.stack([lax.axis_index("rows") % 2, filt // 2, filt % 2]).astype(jnp.int32)
    kernel_flat = kernel.reshape(9 * half, channels)
    planes = 2 * tile_rows

    packed = planes + tile_rows // 2
    same, other, cell_sums = call(
        split_tile,
        [
            ((packed, cells, half), BF16),
            ((packed, cells, half), BF16),
            ((tile_rows // 2, cells, channels), F32),
        ],
        [pltpu.VMEM((2, tile_rows, columns, half), F32)],
        1,
        place,
        features[0],
        cotangent[0],
    )
    packed_same = same
    same, other = swap_tiles((same, other))
    steps = filt_count // 2
    (copies,) = call(
        spread, [((row_count,) + cotangent.shape[1:], BF16)], [], 0, cotangent[0], packed_same, free=(1,)
    )
    cot = lax.all_to_all(copies, "rows", 0, 0, tiled=True).reshape(height, cells, channels)
    act, slope, up = call(
        activate,
        [
            ((2 * planes, cells, half), BF16),
            ((2 * planes, cells, half), F32),
            ((tile_rows, cells, half), F32),
        ],
        [],
        1,
        place,
        same,
        other,
        micros=MU_ACT,
    )
    cot, _ = lax.optimization_barrier((cot, act))
    cross, keep = call(
        back_conv,
        [((steps, 2 * planes, cells, half), BF16), ((steps, 2 * planes, cells, half), F32)],
        [
            pltpu.VMEM(((height + 2) * cells, 4 * channels), BF16),
            pltpu.VMEM((3, 2 * half, 4 * channels), BF16),
            pltpu.VMEM((height, 4, cells, half), F32),
        ],
        1,
        place,
        cot,
        kernel_flat,
        megabytes=20,
        micros=MU_BACK,
    )
    moved = [to_y(act, step) for step in range(1, steps)]
    chunks = []
    for block in [act] + moved:
        chunks += [block, to_core(block)]

    own, *terms = call(
        add_cores,
        [((2 * planes, cells, half), F32)] + [((2 * planes, cells, half), BF16)] * (steps - 1),
        [],
        0,
        keep,
        to_core(cross),
    )
    terms = [to_y(term, step) for step, term in enumerate(terms, 1)]
    conv, kernel_term, outgoing = call(
        forward,
        [
            ((height, cells, channels), BF16),
            ((9 * half, channels), F32),
            ((9 * half, channels), BF16),
        ],
        [
            pltpu.VMEM((4 * height, cells, half), BF16),
            pltpu.VMEM((height * cells, 9 * half), BF16),
            pltpu.VMEM((height * cells, 9 * half), BF16),
            pltpu.SemaphoreType.DMA((2 * steps,)),
        ],
        1,
        place,
        *chunks,
        cot,
        kernel_flat,
        megabytes=20,
        micros=MU_FWD,
        free=range(1, 1 + 2 * steps),
    )
    own, conv, outgoing = lax.optimization_barrier((own, conv, outgoing))
    arrived = lax.ppermute(outgoing, "rep", [(0, 1), (1, 0)])
    conv = lax.all_to_all(conv, "rows", 0, 0, tiled=True)
    same, other = call(
        input_side,
        [((planes, cells, half), BF16), ((planes, cells, half), BF16)],
        [],
        1,
        place,
        own,
        *terms,
        slope,
        up,
        micros=MU_IN,
    )

    same, other = swap_tiles((same, other))
    (pooled,) = call(
        pool,
        [(cotangent.shape[1:], BF16)],
        [],
        0,
        conv.reshape(row_count, tile_rows // 2, cells, channels),
        cell_sums,
        micros=MU_POOL,
    )
    pooled, same, other = lax.optimization_barrier((pooled, same, other))
    (input_grad,) = call(
        join_tile,
        [(features.shape[1:], BF16)],
        [pltpu.VMEM((tile_rows, columns, half), F32)] * 2,
        1,
        place,
        same,
        other,
        micros=MU_JOIN,
    )
    (kernel_grad,) = call(add_images, [((9 * half, channels), F32)], [], 0, kernel_term, arrived, micros=MU_ADD)
    kernel_grad = kernel_grad.reshape(kernel.shape)
    return (pooled[None], input_grad[None], kernel_grad)


def solution(mesh):
    tiles = P("rep", "rows", None, "filt")
    weights = P(None, None, "rows", "filt")
    return jax.shard_map(
        local,
        mesh=mesh,
        in_specs=(tiles, weights, tiles),
        out_specs=(tiles, tiles, weights),
        check_vma=False,
    )
```

```python
import jax
import jax.numpy as jnp
from jax import lax
from jax.experimental import pallas as pl
from jax.experimental.pallas import tpu as pltpu
from jax.sharding import PartitionSpec as P

MU_ACT = 15
MU_POOL, MU_ADD, MU_JOIN, MU_IN, MU_BACK, MU_FWD = 10, 20, 1, 1, 4, 6
AXES = ("filt", "rows", "rep")
VMEM = pl.BlockSpec(memory_space=pltpu.VMEM)
ANY = pl.BlockSpec(memory_space=pl.ANY)
SMEM = pl.BlockSpec(memory_space=pltpu.SMEM)
F32 = jnp.float32
BF16 = jnp.bfloat16


def call(body, outs, scratch, scalars, *args, megabytes=6, free=(), micros=1):
    return pl.pallas_call(
        body,
        out_shape=[jax.ShapeDtypeStruct(shape, dtype) for shape, dtype in outs],
        in_specs=[SMEM if k < scalars else ANY if k in free else VMEM for k in range(len(args))],
        out_specs=[VMEM] * len(outs),
        scratch_shapes=scratch,
        compiler_params=pltpu.CompilerParams(vmem_limit_bytes=megabytes << 20),
        name=body.__name__,
        cost_estimate=pl.CostEstimate(flops=micros * 10**9, bytes_accessed=micros * 3 * 10**6, transcendentals=0),
    )(*args)


def swap_tiles(pair):
    sizes = [lax.axis_size(axis) for axis in AXES]
    stay, cross = [], []
    for f in range(sizes[0]):
        for r in range(sizes[1]):
            for g in range(sizes[2]):
                a, h = r // 2, r % 2
                source = (f * sizes[1] + r) * sizes[2] + g
                stay.append((source, (a * sizes[1] + 2 * f + h) * sizes[2] + g))
                cross.append((source, (a * sizes[1] + 2 * f + 1 - h) * sizes[2] + g))
    return lax.ppermute(pair[0], AXES, stay), lax.ppermute(pair[1], AXES, cross)


def to_y(block, step):
    count = lax.axis_size("filt")
    return lax.ppermute(block, "filt", [(i, (i + 2 * step) % count) for i in range(count)])


def to_core(block):
    return lax.ppermute(block, "filt", [(i, i ^ 1) for i in range(lax.axis_size("filt"))])


def split_tile(place_ref, feat_ref, cot_ref, same_ref, other_ref, cells_ref, wide_ref):
    odd = place_ref[0] == 1
    rows, columns, channels = feat_ref.shape
    half, cells = channels // 2, columns // 2
    for part in range(2):
        wide_ref[part] = feat_ref[:, :, part * half : (part + 1) * half].astype(F32)
    for m in range(rows // 2):
        totals = [jnp.zeros((cells, half), F32)] * 2
        for a in range(2):
            for b in range(2):
                low, high = (wide_ref[part, 2 * m + a, pl.ds(b, cells, stride=2), :] for part in range(2))
                totals = [totals[0] + low, totals[1] + high]
                same_ref[4 * m + 2 * a + b] = jnp.where(odd, high, low).astype(BF16)
                other_ref[4 * m + 2 * a + b] = jnp.where(odd, low, high).astype(BF16)
        cells_ref[m, :, :half] = totals[0]
        cells_ref[m, :, half:] = totals[1]
        grad = cot_ref[m].astype(F32)
        low, high = grad[:, :half], grad[:, half:]
        same_ref[2 * rows + m] = jnp.where(odd, high, low).astype(BF16)
        other_ref[2 * rows + m] = jnp.where(odd, low, high).astype(BF16)


def spread(cot_ref, packed_ref, copies_ref):
    del packed_ref
    for k in range(copies_ref.shape[0]):
        copies_ref[k] = cot_ref[...]


def activate(place_ref, same_ref, other_ref, act_ref, slope_ref, up_ref):
    odd = place_ref[0] == 1
    count, cells, half = same_ref.shape
    planes = act_ref.shape[0] // 2
    same, other = same_ref[...].astype(F32), other_ref[...].astype(F32)
    first, second = jnp.where(odd, other, same), jnp.where(odd, same, other)
    for t, tile in enumerate((first, second)):
        values = tile[:planes]
        logistic = 1.0 / (1.0 + jnp.exp(-values))
        act_ref[t * planes : (t + 1) * planes] = (values * logistic).astype(BF16)
        slope_ref[t * planes : (t + 1) * planes] = logistic * (1.0 + values * (1.0 - logistic))
        up_ref[t * (planes // 4) : (t + 1) * (planes // 4)] = tile[planes:] * 0.25


def back_conv(place_ref, cot_ref, kernel_ref, cross_ref, keep_ref, left_ref, right_ref, sum_ref):
    height, cells, channels = cot_ref.shape
    half = keep_ref.shape[-1]
    tokens = height * cells
    column = lax.broadcasted_iota(jnp.int32, (tokens, channels), 0) % cells
    wide = cot_ref[...].astype(F32).reshape(tokens, channels)
    before = jnp.where(column == 0, 0.0, pltpu.roll(wide, 1, 0)).astype(BF16)
    after = jnp.where(column == cells - 1, 0.0, pltpu.roll(wide, tokens - 1, 0)).astype(BF16)
    blank = jnp.zeros((cells, 4 * channels), BF16)
    left_ref[0:cells] = blank
    left_ref[tokens + cells : tokens + 2 * cells] = blank
    middle = pl.ds(cells, tokens)
    center = cot_ref[...].reshape(tokens, channels)
    left_ref[middle, 0:channels] = center
    left_ref[middle, channels : 2 * channels] = center
    left_ref[middle, 2 * channels : 3 * channels] = before
    left_ref[middle, 3 * channels : 4 * channels] = after
    empty = jnp.zeros((half, channels), BF16)
    for p in range(3):
        taps = [kernel_ref[(3 * p + q) * half : (3 * p + q + 1) * half, :] for q in range(3)]
        blocks = ((taps[0], taps[1]), (taps[1], taps[2]), (taps[2], empty), (empty, taps[0]))
        for k, block in enumerate(blocks):
            for b in range(2):
                right_ref[p, b * half : (b + 1) * half, k * channels : (k + 1) * channels] = block[b]
    for a in range(2):
        total = None
        for p in range(3):
            start = cells * (1 + ((0, 0, -1), (1, 0, 0))[a][p])
            term = lax.dot_general(
                left_ref[start : start + tokens, :],
                right_ref[p],
                (((1,), (1,)), ((), ())),
                preferred_element_type=F32,
            )
            total = term if total is None else total + term
        total = (total * 0.25).reshape(height, cells, 2 * half)
        for b in range(2):
            sum_ref[:, 2 * a + b] = total[:, :, b * half : (b + 1) * half]
    steps = keep_ref.shape[0]
    y, core = place_ref[1], place_ref[2]
    group = height // (2 * steps)
    for step in range(steps):
        pair = 2 * ((y + step) % steps)
        keep_ref[step] = sum_ref[pl.ds((pair + core) * group, group)].reshape(keep_ref.shape[1:])
        cross_ref[step] = sum_ref[pl.ds((pair + 1 - core) * group, group)].reshape(keep_ref.shape[1:]).astype(BF16)


def add_cores(keep_ref, cross_ref, own_ref, *out_refs):
    own_ref[...] = keep_ref[0] + cross_ref[0].astype(F32)
    for step, out_ref in enumerate(out_refs, 1):
        out_ref[...] = (keep_ref[step] + cross_ref[step].astype(F32)).astype(BF16)


def forward(place_ref, *refs):
    chunks, (kernel_ref, conv_ref, coarse_ref, act_ref, fine_ref, arrived) = refs[:-6], refs[-6:]
    steps = len(chunks) // 2
    planes, cells, half = chunks[0].shape
    height = act_ref.shape[0] // 4
    y, core = place_ref[1], place_ref[2]
    copies = []
    for step in range(steps):
        pair = 2 * ((y + steps - step) % steps)
        for k, tile in ((2 * step, pair + core), (2 * step + 1, pair + 1 - core)):
            copies.append(
                pltpu.make_async_copy(chunks[k], act_ref.at[pl.ds(tile * planes, planes)], arrived.at[k])
            )
    for copy in copies:
        copy.start()
    for copy in copies:
        copy.wait()
    column = lax.broadcasted_iota(jnp.int32, (cells, half), 0)

    def plane(i, a, b):
        return act_ref[4 * i + 2 * a + b].astype(F32)

    def put(i, p, even, odd):
        before = jnp.where(column == 0, 0.0, pltpu.roll(odd, 1, 0))
        after = jnp.where(column == cells - 1, 0.0, pltpu.roll(even, cells - 1, 0))
        rows = pl.ds(pl.multiple_of(i * cells, cells), cells)
        return rows, (before + even, even + odd, odd + after)

    def store(rows, p, sums):
        for q, box in enumerate(sums):
            coarse = box.astype(BF16)
            lanes = slice((3 * p + q) * half, (3 * p + q + 1) * half)
            coarse_ref[rows, lanes] = coarse
            fine_ref[rows, lanes] = (box - coarse.astype(F32)).astype(BF16)

    rows, sums = put(0, 0, plane(0, 0, 0), plane(0, 0, 1))
    store(rows, 0, sums)
    rows, sums = put(height - 1, 2, plane(height - 1, 1, 0), plane(height - 1, 1, 1))
    store(rows, 2, sums)

    def whole(i, _):
        rows, sums = put(i, 1, plane(i, 0, 0) + plane(i, 1, 0), plane(i, 0, 1) + plane(i, 1, 1))
        store(rows, 1, sums)
        return 0

    def between(i, _):
        rows, sums = put(
            i, 0, plane(i - 1, 1, 0) + plane(i, 0, 0), plane(i - 1, 1, 1) + plane(i, 0, 1)
        )
        store(rows, 0, sums)
        store(pl.ds(pl.multiple_of((i - 1) * cells, cells), cells), 2, sums)
        return 0

    lax.fori_loop(0, height, whole, 0, unroll=4)
    lax.fori_loop(1, height, between, 0, unroll=4)

    conv = jnp.dot(coarse_ref[...], kernel_ref[...], preferred_element_type=F32)
    conv = conv + jnp.dot(fine_ref[...], kernel_ref[...], preferred_element_type=F32)
    conv_ref[...] = conv.astype(BF16).reshape(conv_ref.shape)


def kernel_side(coarse_ref, cot_ref, keep_ref, send_ref):
    grad = lax.dot_general(
        coarse_ref[...],
        cot_ref[...].reshape(coarse_ref.shape[0], -1),
        (((0,), (0,)), ((), ())),
        preferred_element_type=F32,
    ) * 0.25
    keep_ref[...] = grad
    send_ref[...] = grad.astype(BF16)


def input_side(place_ref, own_ref, *refs):
    terms, (slope_ref, up_ref, same_ref, other_ref) = refs[:-4], refs[-4:]
    odd = place_ref[0] == 1
    planes = same_ref.shape[0]
    grads = []
    for t in range(2):
        block = slice(t * planes, (t + 1) * planes)
        total = own_ref[block]
        for term in terms:
            total = total + term[block].astype(F32)
        total = total * slope_ref[block]
        up = up_ref[t * (planes // 4) : (t + 1) * (planes // 4)]
        grads.append([total[k] + up[k // 4] for k in range(planes)])
    for k in range(planes):
        same_ref[k] = jnp.where(odd, grads[1][k], grads[0][k]).astype(BF16)
        other_ref[k] = jnp.where(odd, grads[0][k], grads[1][k]).astype(BF16)


def pool(conv_ref, cells_ref, out_ref):
    total = cells_ref[...]
    for k in range(conv_ref.shape[0]):
        total = total + conv_ref[k].astype(F32)
    out_ref[...] = (total * 0.25).astype(BF16)


def add_images(keep_ref, arrived_ref, out_ref):
    out_ref[...] = keep_ref[...] + arrived_ref[...].astype(F32)


def join_tile(place_ref, same_ref, other_ref, out_ref, low_ref, high_ref):
    odd = place_ref[0] == 1
    rows, columns, channels = out_ref.shape
    half = channels // 2
    for k in range(2 * rows):
        row, b = 2 * (k // 4) + (k // 2) % 2, k % 2
        same, other = same_ref[k].astype(F32), other_ref[k].astype(F32)
        low_ref[row, pl.ds(b, columns // 2, stride=2), :] = jnp.where(odd, other, same)
        high_ref[row, pl.ds(b, columns // 2, stride=2), :] = jnp.where(odd, same, other)
    out_ref[:, :, :half] = low_ref[...].astype(BF16)
    out_ref[:, :, half:] = high_ref[...].astype(BF16)


def local(features, kernel, cotangent):
    tile_rows, columns, channels = features.shape[1:]
    half, cells = channels // 2, columns // 2
    filt_count, row_count = lax.axis_size("filt"), lax.axis_size("rows")
    height = tile_rows * row_count // 2
    filt = lax.axis_index("filt")
    place = jnp.stack([lax.axis_index("rows") % 2, filt // 2, filt % 2]).astype(jnp.int32)
    kernel_flat = kernel.reshape(9 * half, channels)
    planes = 2 * tile_rows

    packed = planes + tile_rows // 2
    same, other, cell_sums = call(
        split_tile,
        [
            ((packed, cells, half), BF16),
            ((packed, cells, half), BF16),
            ((tile_rows // 2, cells, channels), F32),
        ],
        [pltpu.VMEM((2, tile_rows, columns, half), F32)],
        1,
        place,
        features[0],
        cotangent[0],
    )
    packed_same = same
    same, other = swap_tiles((same, other))
    steps = filt_count // 2
    (copies,) = call(
        spread, [((row_count,) + cotangent.shape[1:], BF16)], [], 0, cotangent[0], packed_same, free=(1,)
    )
    cot = lax.all_to_all(copies, "rows", 0, 0, tiled=True).reshape(height, cells, channels)
    act, slope, up = call(
        activate,
        [
            ((2 * planes, cells, half), BF16),
            ((2 * planes, cells, half), F32),
            ((tile_rows, cells, half), F32),
        ],
        [],
        1,
        place,
        same,
        other,
        micros=MU_ACT,
    )
    moved = [to_y(act, step) for step in range(1, steps)]
    chunks = []
    for block in [act] + moved:
        chunks += [block, to_core(block)]
    conv, coarse = call(
        forward,
        [((height, cells, channels), BF16), ((height * cells, 9 * half), BF16)],
        [
            pltpu.VMEM((4 * height, cells, half), BF16),
            pltpu.VMEM((height * cells, 9 * half), BF16),
            pltpu.SemaphoreType.DMA((2 * steps,)),
        ],
        1,
        place,
        *chunks,
        kernel_flat,
        megabytes=20,
        micros=MU_FWD,
        free=range(1, 1 + 2 * steps),
    )
    cot, _ = lax.optimization_barrier((cot, conv))
    cross, keep = call(
        back_conv,
        [((steps, 2 * planes, cells, half), BF16), ((steps, 2 * planes, cells, half), F32)],
        [
            pltpu.VMEM(((height + 2) * cells, 4 * channels), BF16),
            pltpu.VMEM((3, 2 * half, 4 * channels), BF16),
            pltpu.VMEM((height, 4, cells, half), F32),
        ],
        1,
        place,
        cot,
        kernel_flat,
        megabytes=20,
        micros=MU_BACK,
    )
    own, *terms = call(
        add_cores,
        [((2 * planes, cells, half), F32)] + [((2 * planes, cells, half), BF16)] * (steps - 1),
        [],
        0,
        keep,
        to_core(cross),
    )
    terms = [to_y(term, step) for step, term in enumerate(terms, 1)]
    kernel_term, outgoing = call(
        kernel_side,
        [((9 * half, channels), F32), ((9 * half, channels), BF16)],
        [],
        0,
        coarse,
        cot,
        megabytes=20,
    )
    own, conv, outgoing = lax.optimization_barrier((own, conv, outgoing))
    arrived = lax.ppermute(outgoing, "rep", [(0, 1), (1, 0)])
    conv = lax.all_to_all(conv, "rows", 0, 0, tiled=True)
    same, other = call(
        input_side,
        [((planes, cells, half), BF16), ((planes, cells, half), BF16)],
        [],
        1,
        place,
        own,
        *terms,
        slope,
        up,
        micros=MU_IN,
    )

    same, other = swap_tiles((same, other))
    (pooled,) = call(
        pool,
        [(cotangent.shape[1:], BF16)],
        [],
        0,
        conv.reshape(row_count, tile_rows // 2, cells, channels),
        cell_sums,
        micros=MU_POOL,
    )
    pooled, same, other = lax.optimization_barrier((pooled, same, other))
    (input_grad,) = call(
        join_tile,
        [(features.shape[1:], BF16)],
        [pltpu.VMEM((tile_rows, columns, half), F32)] * 2,
        1,
        place,
        same,
        other,
        micros=MU_JOIN,
    )
    (kernel_grad,) = call(add_images, [((9 * half, channels), F32)], [], 0, kernel_term, arrived, micros=MU_ADD)
    kernel_grad = kernel_grad.reshape(kernel.shape)
    return (pooled[None], input_grad[None], kernel_grad)


def solution(mesh):
    tiles = P("rep", "rows", None, "filt")
    weights = P(None, None, "rows", "filt")
    return jax.shard_map(
        local,
        mesh=mesh,
        in_specs=(tiles, weights, tiles),
        out_specs=(tiles, tiles, weights),
        check_vma=False,
    )
```
